128 devices in a mesh: dp: 8 (over y_hi, x), tensor: 16 (over y_lo, z, core).
Axes of the slice: x: 4, y: 4 (y_hi: 2, y_lo: 2; y = y_hi * 2 + y_lo), z: 4, core: 2. Of those that a mesh axis runs over, the one named last changes fastest.
Arguments:
- tokens: bfloat16 [32768, 6144], P(('dp', 'tensor')), may hold values from -6 to 6
- expert_ids: int32 [32768, 2], P(('dp', 'tensor')), may hold values from 0 to 7, as said below
- slot_ids: int32 [32768, 2], P(('dp', 'tensor')), may hold values from 0 to 64, as said below
- gate_probs: float32 [32768, 2], P(('dp', 'tensor')), may hold values from 0.05 to 0.95
- gate_weight: bfloat16 [6144, 8192], P('dp', 'tensor'), may hold values from -0.078125 to 0.078125
- up_weight: bfloat16 [6144, 8192], P('dp', 'tensor'), may hold values from -0.078125 to 0.078125
- down_weight: bfloat16 [8192, 6144], P('tensor', 'dp'), may hold values from -0.0625 to 0.0625
Outputs:
- mixed: bfloat16 [32768, 6144], P(('dp', 'tensor'))
The draws below stay inside these ranges and needn't reach their ends.
Inputs may be any that keep to these rules, and one draw needn't show every extreme that they name: `expert_ids`: each row names 2 different experts. slot_ids[t, k] counts the tokens before t in t's run of 256 that name expert expert_ids[t, k]; a count of 64 or more is given as 64, and then the token is left out of that expert's group. In some window every run has more than 64 tokens naming expert 0.
All inputs are finite; a program needn't handle non-finite values.
Results may differ from the reference program's by a relative error of at most 0.024.
Values may be sent and summed in bfloat16 or wider, within the bound.
A program may use at most 128 MiB of HBM per device.

```python
from functools import partial
import jax
import jax.numpy as jnp
from jax import lax

D = 6144
EXPERTS = 8
TOPK = 2
FF = 8192
SEQ_DEV = 256
C_DEV = 64
SLIVER = 512
WINDOW = 4096
CAP = 1024
TOKENS = 32768
N_DP = 8
N_TENSOR = 16


def route_tables(key):
    blocks = TOKENS // SEQ_DEV
    keys = jax.random.split(key, 6)
    highest = C_DEV + C_DEV // 4
    counts = jax.random.randint(keys[0], (blocks,), C_DEV // 2, highest + 1)
    full_window = jax.random.randint(keys[1], (), 0, TOKENS // WINDOW)
    window_of = jnp.arange(blocks) // (WINDOW // SEQ_DEV)
    counts = jnp.where(window_of == full_window, highest, counts)
    ranks = jax.vmap(lambda sub_key: jax.random.permutation(sub_key, SEQ_DEV))(jax.random.split(keys[2], blocks))
    chosen = ranks < counts[:, None]
    placing = jax.random.randint(keys[3], (blocks, SEQ_DEV), 0, 2)
    first_id = jax.random.randint(keys[4], (blocks, SEQ_DEV), 1, EXPERTS)
    step_id = jax.random.randint(keys[5], (blocks, SEQ_DEV), 1, EXPERTS - 1)
    second_id = 1 + (first_id - 1 + step_id) % (EXPERTS - 1)
    column_one = jnp.where(chosen, jnp.where(placing == 0, 0, first_id), first_id)
    column_two = jnp.where(chosen, jnp.where(placing == 0, first_id, 0), second_id)
    id_table = jnp.stack([column_one, column_two], axis=-1).astype(jnp.int32)
    onehot = (id_table[..., None] == jnp.arange(EXPERTS)[None, None, None, :]).astype(jnp.int32)
    per_token = jnp.sum(onehot, axis=2)
    earlier = jnp.cumsum(per_token, axis=1) - per_token
    slot_table = jnp.sum(onehot * earlier[:, :, None, :], axis=3)
    slot_table = jnp.minimum(slot_table, C_DEV).astype(jnp.int32)
    return (id_table.reshape(TOKENS, 2), slot_table.reshape(TOKENS, 2))


def draw_expert_ids(key, part):
    id_table, slot_table = route_tables(key)
    return id_table


def draw_slot_ids(key, part):
    id_table, slot_table = route_tables(key)
    return slot_table


def block_scale(rng, shape, cuts, smallest, top_value):
    gain, own = 1.0, jax.random.fold_in(rng, 6)
    for position, parts in cuts:
        draws = jnp.exp(jax.random.uniform(jax.random.fold_in(own, position), (parts,), jnp.float32, smallest / len(cuts), top_value / len(cuts)))
        gain = gain * jnp.repeat(draws, shape[position] // parts).reshape([-1 if axis == position else 1 for axis in range(len(shape))])
    return gain


def gaussian(key, extent, width, reach, pieces=(), kind=jnp.bfloat16):
    entries = jax.random.normal(key, extent, jnp.float32) * width
    if len(pieces) > 0:
        entries = block_scale(key, extent, pieces, -0.22, 0.18) * entries
    return jnp.clip(entries, min=-reach, max=reach).astype(kind)


def setup_inputs(seed: int = 0) -> dict:
    key_list = jax.random.split(jax.random.key(seed), 8)
    tokens = gaussian(key_list[0], (TOKENS, D), 1.0, 6.0, ((0, 128),))
    expert_ids = draw_expert_ids(jax.random.fold_in(key_list[7], 71), 0)
    slot_ids = draw_slot_ids(jax.random.fold_in(key_list[7], 71), 0)
    gate_probs = jnp.clip(0.05 + 0.9 * jax.random.uniform(key_list[3], (TOKENS, TOPK), jnp.float32) ** block_scale(key_list[3], (TOKENS, TOPK), ((0, 128),), -0.2, 0.2), 0.05, 0.95)
    gate_weight = gaussian(key_list[4], (D, FF), D ** -0.5, 0.078125, ((0, 8), (1, 16)))
    up_weight = gaussian(key_list[5], (D, FF), D ** -0.5, 0.078125, ((0, 8), (1, 16)))
    down_weight = gaussian(key_list[6], (FF, D), FF ** -0.5, 0.0625, ((0, 16), (1, 8)))
    return dict(tokens=tokens, expert_ids=expert_ids, slot_ids=slot_ids, gate_probs=gate_probs, gate_weight=gate_weight, up_weight=up_weight, down_weight=down_weight)


def window_output(inputs, gate_weight, up_weight, down_weight):
    window_tokens, target, weight_used = inputs
    group_rows = jnp.zeros((CAP, D), jnp.bfloat16).at[target].set(window_tokens, mode="drop")
    gate_sum = jnp.dot(group_rows, gate_weight, preferred_element_type=jnp.float32)
    up_sum = jnp.dot(group_rows, up_weight, preferred_element_type=jnp.float32)
    hidden = (jax.nn.silu(gate_sum) * up_sum).astype(jnp.bfloat16)

    def add_sliver(sliver_index, running):
        offset = (sliver_index * SLIVER).astype(jnp.int32)
        hidden_part = lax.dynamic_slice_in_dim(hidden, offset, SLIVER, 1)
        weight_part = lax.dynamic_slice_in_dim(down_weight, offset, SLIVER, 0)
        partial_sum = jnp.dot(hidden_part, weight_part, preferred_element_type=jnp.float32).astype(jnp.bfloat16)
        partial_sum = lax.optimization_barrier(partial_sum)
        return running + partial_sum.astype(jnp.float32)

    expert_rows = lax.fori_loop(0, N_TENSOR, add_sliver, jnp.zeros((CAP, D), jnp.float32))
    picked = expert_rows[jnp.minimum(target, CAP - 1)]
    return (picked * weight_used[:, None]).astype(jnp.bfloat16)


def reference(tokens, expert_ids, slot_ids, gate_probs, gate_weight, up_weight, down_weight):
    expert_hits = expert_ids == 0
    slot_used = jnp.min(jnp.where(expert_hits, slot_ids, C_DEV), axis=1).astype(jnp.int32)
    weight_used = jnp.sum(jnp.where(expert_hits, gate_probs, jnp.zeros_like(gate_probs)), axis=1)
    weight_used = jnp.where(slot_used < C_DEV, weight_used, jnp.zeros_like(weight_used))
    device_of = ((jnp.arange(TOKENS, dtype=jnp.int32) // SEQ_DEV) % N_TENSOR).astype(jnp.int32)
    target = jnp.where(slot_used < C_DEV, device_of * C_DEV + slot_used, CAP).astype(jnp.int32)
    shaped = (tokens.reshape(N_DP, WINDOW, D), target.reshape(N_DP, WINDOW), weight_used.reshape(N_DP, WINDOW))
    outputs = lax.map(partial(window_output, gate_weight=gate_weight, up_weight=up_weight, down_weight=down_weight), shaped)
    return outputs.reshape(TOKENS, D)
```

```python
import functools

import jax
import jax.numpy as jnp
from jax import lax
from jax.experimental import pallas as pl
from jax.experimental.pallas import tpu as pltpu
from jax.sharding import PartitionSpec as P

MESH = pl.DeviceIdType.MESH
F32 = jnp.float32
BF16 = jnp.bfloat16

SLOTS = 64
RUN = 256
DEPTH = 768
UNITS = 512
ROWS = 1024
SHARDS = 8
SPLIT = 512
COPIES = 112

ORDER = (0, 4, 1, 3, 5, 7, 2, 6)


def place():
    dp, tensor = lax.axis_index("dp"), lax.axis_index("tensor")
    return dp // 4, dp % 4, tensor // 8, (tensor // 2) % 4, tensor % 2


def device(d_yh, d_x, d_yl, d_z, d_c):
    yh, x, yl, z, c = place()
    yh, x, yl, z, c = (yh + d_yh) % 2, (x + d_x) % 4, (yl + d_yl) % 2, (z + d_z) % 4, (c + d_c) % 2
    return (yh * 4 + x, yl * 8 + z * 2 + c)


def shard_columns(s):
    yh, x, _, _, _ = place()
    owner = ((yh + s // 4) % 2) * 4 + (x + s % 4) % 4
    return pl.ds(pl.multiple_of(owner * DEPTH, DEPTH), DEPTH)


def kernel(
    tok_hbm, ids_ref, slots_ref, probs_ref, wg_hbm, wu_hbm, wd_hbm, out_hbm,
    xbuf, wg, wu, wd, accg, accu, hid, c1r, z2r, z1r, q, f0, yr, ost, send_sem, recv_sem, local_sem,
):
    XP, XM = device(0, 1, 0, 0, 0), device(0, 3, 0, 0, 0)
    Y2, YN = device(1, 0, 0, 0, 0), device(0, 0, 1, 0, 0)
    ZP, ZM = device(0, 0, 0, 1, 0), device(0, 0, 0, 3, 0)
    CORE = device(0, 0, 0, 0, 1)
    started = []

    def send(src, dst, to):
        i = len(started)
        copy = pltpu.make_async_remote_copy(
            src_ref=src, dst_ref=dst, send_sem=send_sem.at[i], recv_sem=recv_sem.at[i],
            device_id=to, device_id_type=MESH,
        )
        copy.start()
        started.append(copy)
        return copy

    tok_loads = []
    for s in range(SHARDS):
        load = pltpu.make_async_copy(tok_hbm.at[:, shard_columns(s)], c1r.at[s, pl.ds(0, RUN)], local_sem.at[s])
        load.start()
        tok_loads.append(load)
    own_loads = []
    for k, (src, dst) in enumerate(((wg_hbm, wg), (wu_hbm, wu), (wd_hbm, wd))):
        load = pltpu.make_async_copy(src, dst.at[0], local_sem.at[8 + k])
        load.start()
        own_loads.append(load)

    barrier = pltpu.get_barrier_semaphore()
    for to in (XP, XM, Y2, YN, ZP, ZM, CORE):
        pl.semaphore_signal(barrier, inc=1, device_id=to, device_id_type=MESH)
    pl.semaphore_wait(barrier, 7)

    g_x = (send(wg_hbm, wg.at[3], XP), send(wg_hbm, wg.at[1], XM))
    u_x = (send(wu_hbm, wu.at[3], XP), send(wu_hbm, wu.at[1], XM))

    hit0, hit1 = ids_ref[:, 0:1] == 0, ids_ref[:, 1:2] == 0
    slot = jnp.minimum(
        jnp.where(hit0, slots_ref[:, 0:1], SLOTS), jnp.where(hit1, slots_ref[:, 1:2], SLOTS)
    )
    weight = jnp.where(hit0, probs_ref[:, 0:1], 0.0) + jnp.where(hit1, probs_ref[:, 1:2], 0.0)
    lane = lax.broadcasted_iota(jnp.int32, (RUN, 2 * SLOTS), 1)
    lane = jnp.where(lane >= SLOTS, lane - SLOTS, lane)
    picker = jnp.where(lane == slot, 1.0, 0.0)
    picker_t = picker.T[:SLOTS].astype(BF16)
    for s in range(SHARDS):
        tok_loads[s].wait()
        xbuf[s, pl.ds(0, SLOTS), :] = jnp.dot(
            picker_t, c1r[s, pl.ds(0, RUN), :], preferred_element_type=F32
        ).astype(BF16)

    def block(rc, ryl, rz, half=None):
        at = pl.ds(rc * 512 + ryl * 256 + rz * 64, 64)
        if half is None:
            return xbuf.at[:, at]
        return xbuf.at[pl.ds(half * 4, 4), at]

    to_core = []

    def core(ryl, rz, half=None):
        to_core.append(send(block(0, ryl, rz, half), block(1, ryl, rz, half), CORE))

    x_y = send(block(0, 0, 0), block(0, 1, 0), YN)
    x_z = (send(block(0, 0, 0), block(0, 0, 3), ZP), send(block(0, 0, 0), block(0, 0, 1), ZM))
    core(0, 0)
    g_y = send(wg_hbm, wg.at[4], Y2)
    u_y = send(wu_hbm, wu.at[4], Y2)

    lo, hi = pl.ds(0, 384), pl.ds(384, 384)
    ring, rest = pl.ds(0, SPLIT), pl.ds(SPLIT, DEPTH - SPLIT)
    ring_lo, ring_hi = pl.ds(0, SPLIT // 2), pl.ds(SPLIT // 2, SPLIT // 2)

    def relay_own(w, first):
        first[0].wait_recv()
        a = send(w.at[3, lo], w.at[2, lo], XP)
        first[1].wait_recv()
        b = send(w.at[1, hi], w.at[2, hi], XM)
        c = send(w.at[3, rest], w.at[7, rest], Y2)
        d = send(w.at[1, rest], w.at[5, rest], Y2)
        return a, b, c, d

    def ring_partner(w, first):
        first.wait_recv()
        return send(w.at[4, ring], w.at[7, ring], XP), send(w.at[4, ring], w.at[5, ring], XM)

    def relay_partner(w, first):
        first[0].wait_recv()
        a = send(w.at[7, ring_lo], w.at[6, ring_lo], XP)
        first[1].wait_recv()
        return a, send(w.at[5, ring_hi], w.at[6, ring_hi], XM)

    g_r = relay_own(wg, g_x)
    x_z[0].wait_recv()
    x_zr = [send(block(0, 0, 3, 0), block(0, 0, 2, 0), ZP)]
    core(0, 3)
    x_z[1].wait_recv()
    x_zr.append(send(block(0, 0, 1, 1), block(0, 0, 2, 1), ZM))
    core(0, 1)
    x_y.wait_recv()
    x_yz = (send(block(0, 1, 0), block(0, 1, 3), ZP), send(block(0, 1, 0), block(0, 1, 1), ZM))
    core(1, 0)
    g_p = ring_partner(wg, g_y)
    for half in (0, 1):
        x_zr[half].wait_recv()
        core(0, 2, half)
    u_r = relay_own(wu, u_x)
    x_yz[0].wait_recv()
    x_yzr = [send(block(0, 1, 3, 0), block(0, 1, 2, 0), ZP)]
    core(1, 3)
    x_yz[1].wait_recv()
    x_yzr.append(send(block(0, 1, 1, 1), block(0, 1, 2, 1), ZM))
    core(1, 1)

    def far_rest(w, relays):
        relays[0].wait_recv()
        relays[1].wait_recv()
        return send(w.at[2, rest], w.at[6, rest], Y2)

    g_f = far_rest(wg, g_r)
    u_p = ring_partner(wu, u_y)
    for half in (0, 1):
        x_yzr[half].wait_recv()
        core(1, 2, half)
    u_f = far_rest(wu, u_r)
    d_y = send(wd_hbm, wd.at[4], Y2)
    for copy in to_core:
        copy.wait_recv()

    def gemm(acc, w, s, first=False):
        @pl.loop(0, 2)
        def _(m):
            rows = pl.ds(pl.multiple_of(m * 512, 512), 512)
            part = jnp.dot(xbuf[s, rows, :], w[s], preferred_element_type=F32)
            if first:
                acc[rows, :] = part
            else:
                acc[rows, :] += part

    own_loads[0].wait()
    own_loads[1].wait()
    gemm(accg, wg, 0, True)
    gemm(accu, wu, 0, True)
    gemm(accg, wg, 1)
    gemm(accg, wg, 3)
    gemm(accg, wg, 4)
    gemm(accg, wg, 2)
    g_pr = relay_partner(wg, g_p)
    gemm(accu, wu, 1)
    gemm(accu, wu, 3)
    gemm(accu, wu, 4)
    gemm(accu, wu, 2)
    u_pr = relay_partner(wu, u_p)
    d_x = (send(wd_hbm, wd.at[3], XP), send(wd_hbm, wd.at[1], XM))
    d_y.wait_recv()
    d_p = (send(wd.at[4], wd.at[7], XP), send(wd.at[4], wd.at[5], XM))
    g_r[2].wait_recv()
    gemm(accg, wg, 7)
    g_r[3].wait_recv()
    gemm(accg, wg, 5)
    u_r[2].wait_recv()
    gemm(accu, wu, 7)
    u_r[3].wait_recv()
    gemm(accu, wu, 5)
    for copy in (g_f, *g_pr):
        copy.wait_recv()
    gemm(accg, wg, 6)
    for copy in (u_f, *u_pr):
        copy.wait_recv()
    gemm(accu, wu, 6)

    @pl.loop(0, 4)
    def _(m):
        rows = pl.ds(pl.multiple_of(m * 256, 256), 256)
        gate = accg[rows, :]
        hid[rows, :] = (gate / (1.0 + jnp.exp(-gate)) * accu[rows, :]).astype(BF16)

    for copy in (x_y, *x_z, *x_zr, *x_yz, *x_yzr, *to_core):
        copy.wait_send()

    d_lo, d_hi = pl.ds(0, 256), pl.ds(256, 256)
    c1, z2, z1, y1, outs = {}, {}, {}, {}, {}
    d_r, d_pr = [], []

    def down_ready(s):
        if s == 0:
            own_loads[2].wait()
        elif s == 1:
            d_x[0].wait_recv()
            d_x[1].wait_recv()
            d_r.append(send(wd.at[3, d_lo], wd.at[2, d_lo], XP))
            d_r.append(send(wd.at[1, d_hi], wd.at[2, d_hi], XM))
        elif s == 5:
            d_p[0].wait_recv()
            d_p[1].wait_recv()
            d_pr.append(send(wd.at[7, d_lo], wd.at[6, d_lo], XP))
            d_pr.append(send(wd.at[5, d_hi], wd.at[6, d_hi], XM))
        elif s == 2:
            for copy in d_r:
                copy.wait_recv()
        elif s == 6:
            for copy in d_pr:
                copy.wait_recv()

    def step_core(s):
        down_ready(s)

        @pl.loop(0, 2)
        def _(m):
            rows = pl.ds(pl.multiple_of(512 + m * 256, 256), 256)
            xbuf[s, rows, :] = jnp.dot(hid[rows, :], wd[s], preferred_element_type=F32).astype(BF16)

        c1[s] = send(xbuf.at[s, pl.ds(512, 512)], c1r.at[s], CORE)

    def step_far(i, s):
        c1[s].wait_recv()

        @pl.loop(0, 2)
        def _(m):
            rows = pl.ds(pl.multiple_of(m * 256, 256), 256)
            at = pl.ds(pl.multiple_of(m * 64, 64), 64)
            part = jnp.dot(hid[rows, :], wd[s], preferred_element_type=F32) + c1r[s, rows, :].astype(F32)
            q[i % 3, 0, at, :] = part[0:64]
            q[i % 3, 1, at, :] = part[64:128]
            q[i % 3, 2, at, :] = part[192:256]
            xbuf[s, pl.ds(pl.multiple_of(256 + m * 64, 64), 64), :] = part[128:192].astype(BF16)

        z2[s] = (
            send(xbuf.at[s, pl.ds(256, 128), lo], z2r.at[s, 0], ZP),
            send(xbuf.at[s, pl.ds(256, 128), hi], z2r.at[s, 1], ZM),
        )

    def step_near(i, s):
        z2[s][0].wait_recv()
        z2[s][1].wait_recv()
        xbuf[s, 0:128, 0:384] = (q[i % 3, 1, :, 0:384] + z2r[s, 0].astype(F32)).astype(BF16)
        xbuf[s, 0:128, 384:768] = q[i % 3, 1, :, 384:768].astype(BF16)
        xbuf[s, 128:256, 0:384] = q[i % 3, 2, :, 0:384].astype(BF16)
        xbuf[s, 128:256, 384:768] = (q[i % 3, 2, :, 384:768] + z2r[s, 1].astype(F32)).astype(BF16)
        z1[s] = (
            send(xbuf.at[s, pl.ds(0, 128)], z1r.at[s, 0], ZP),
            send(xbuf.at[s, pl.ds(128, 128)], z1r.at[s, 1], ZM),
        )

    def step_y(i, s):
        z1[s][0].wait_recv()
        z1[s][1].wait_recv()
        total = q[i % 3, 0] + z1r[s, 0].astype(F32) + z1r[s, 1].astype(F32)
        f0[i % 2] = total[0:64]
        xbuf[s, 384:448, :] = total[64:128].astype(BF16)
        y1[s] = send(xbuf.at[s, pl.ds(384, 64)], yr.at[s], YN)

    def step_out(i, s):
        y1[s].wait_recv()
        rows = f0[i % 2] + yr[s].astype(F32)
        head = rows.astype(BF16)
        tail = (rows - head.astype(F32)).astype(BF16)
        mixed = weight * jnp.dot(
            picker.astype(BF16), jnp.concatenate([head, tail], axis=0), preferred_element_type=F32
        )
        if i >= 2:
            outs[i - 2].wait()
        ost[i % 2] = mixed.astype(BF16)
        outs[i] = pltpu.make_async_copy(ost.at[i % 2], out_hbm.at[:, shard_columns(s)], local_sem.at[11 + i])
        outs[i].start()

    for i in range(SHARDS + 4):
        if i < SHARDS:
            step_core(ORDER[i])
        if 0 <= i - 1 < SHARDS:
            step_far(i - 1, ORDER[i - 1])
        if 0 <= i - 2 < SHARDS:
            step_near(i - 2, ORDER[i - 2])
        if 0 <= i - 3 < SHARDS:
            step_y(i - 3, ORDER[i - 3])
        if 0 <= i - 4 < SHARDS:
            step_out(i - 4, ORDER[i - 4])

    outs[SHARDS - 2].wait()
    outs[SHARDS - 1].wait()
    waited = (x_y, *x_z, *x_zr, *x_yz, *x_yzr, *to_core)
    for copy in started:
        if not any(copy is other for other in waited):
            copy.wait_send()


def body(tokens, expert_ids, slot_ids, gate_probs, gate_weight, up_weight, down_weight):
    hbm, vmem = pl.BlockSpec(memory_space=pl.ANY), pl.BlockSpec(memory_space=pltpu.VMEM)
    return pl.pallas_call(
        kernel,
        out_shape=jax.ShapeDtypeStruct(tokens.shape, BF16),
        in_specs=[hbm, vmem, vmem, vmem, hbm, hbm, hbm],
        out_specs=hbm,
        scratch_shapes=[
            pltpu.VMEM((SHARDS, ROWS, DEPTH), BF16),
            pltpu.VMEM((SHARDS, DEPTH, UNITS), BF16),
            pltpu.VMEM((SHARDS, DEPTH, UNITS), BF16),
            pltpu.VMEM((SHARDS, UNITS, DEPTH), BF16),
            pltpu.VMEM((ROWS, UNITS), F32),
            pltpu.VMEM((ROWS, UNITS), F32),
            pltpu.VMEM((ROWS, UNITS), BF16),
            pltpu.VMEM((SHARDS, 512, DEPTH), BF16),
            pltpu.VMEM((SHARDS, 2, 128, 384), BF16),
            pltpu.VMEM((SHARDS, 2, 128, DEPTH), BF16),
            pltpu.VMEM((3, 3, 128, DEPTH), F32),
            pltpu.VMEM((2, SLOTS, DEPTH), F32),
            pltpu.VMEM((SHARDS, SLOTS, DEPTH), BF16),
            pltpu.VMEM((2, RUN, DEPTH), BF16),
            pltpu.SemaphoreType.DMA((COPIES,)),
            pltpu.SemaphoreType.DMA((COPIES,)),
            pltpu.SemaphoreType.DMA((20,)),
        ],
        compiler_params=pltpu.CompilerParams(
            collective_id=0, has_side_effects=True, vmem_limit_bytes=62 << 20
        ),
        cost_estimate=pl.CostEstimate(flops=20_000_000_000, bytes_accessed=60_000_000, transcendentals=1_000_000),
    )(tokens, expert_ids, slot_ids, gate_probs, gate_weight, up_weight, down_weight)


def solution(mesh):
    return jax.shard_map(
        body,
        mesh=mesh,
        in_specs=(
            P(("dp", "tensor"), None),
            P(("dp", "tensor"), None),
            P(("dp", "tensor"), None),
            P(("dp", "tensor"), None),
            P("dp", "tensor"),
            P("dp", "tensor"),
            P("tensor", "dp"),
        ),
        out_specs=P(("dp", "tensor"), None),
        check_vma=False,
    )
```

```python
import functools

import jax
import jax.numpy as jnp
from jax import lax
from jax.experimental import pallas as pl
from jax.experimental.pallas import tpu as pltpu
from jax.sharding import PartitionSpec as P

MESH = pl.DeviceIdType.MESH
F32 = jnp.float32
BF16 = jnp.bfloat16

SLOTS = 64
RUN = 256
DEPTH = 768
UNITS = 512
ROWS = 1024
SHARDS = 8
SPLIT = 528
COPIES = 112

ORDER = (0, 4, 1, 3, 5, 7, 2, 6)


def place():
    dp, tensor = lax.axis_index("dp"), lax.axis_index("tensor")
    return dp // 4, dp % 4, tensor // 8, (tensor // 2) % 4, tensor % 2


def device(d_yh, d_x, d_yl, d_z, d_c):
    yh, x, yl, z, c = place()
    yh, x, yl, z, c = (yh + d_yh) % 2, (x + d_x) % 4, (yl + d_yl) % 2, (z + d_z) % 4, (c + d_c) % 2
    return (yh * 4 + x, yl * 8 + z * 2 + c)


def shard_columns(s):
    yh, x, _, _, _ = place()
    owner = ((yh + s // 4) % 2) * 4 + (x + s % 4) % 4
    return pl.ds(pl.multiple_of(owner * DEPTH, DEPTH), DEPTH)


def slot_row(ids_ref, slots_ref):
    first = jnp.where(ids_ref[0:1, :] == 0, slots_ref[0:1, :], SLOTS)
    return jnp.minimum(first, jnp.where(ids_ref[1:2, :] == 0, slots_ref[1:2, :], SLOTS))


def combine(ids_ref, slots_ref, probs_ref, rows_ref, mixed_ref):
    row = lax.broadcasted_iota(jnp.int32, (2 * SLOTS, RUN), 0)
    row = jnp.where(row >= SLOTS, row - SLOTS, row)
    picked = row == slot_row(ids_ref, slots_ref)
    weight = jnp.where(ids_ref[0:1, :] == 0, probs_ref[0:1, :], 0.0)
    weight += jnp.where(ids_ref[1:2, :] == 0, probs_ref[1:2, :], 0.0)
    picker = jnp.where(picked, 1.0, 0.0).T.astype(BF16)
    weight = jnp.sum(jnp.where(picked, weight, 0.0).T[:, :SLOTS], axis=1, keepdims=True)
    rows = rows_ref[...]
    head = rows.astype(BF16)
    tail = (rows - head.astype(F32)).astype(BF16)
    both = jnp.concatenate([head, tail], axis=0)
    mixed_ref[...] = (weight * jnp.dot(picker, both, preferred_element_type=F32)).astype(BF16)


def kernel(
    tok_hbm, ids_ref, slots_ref, wg_hbm, wu_hbm, wd_hbm, out_hbm,
    xbuf, wg, wu, wd, accg, accu, hid, c1r, z2r, z1r, q, f0, yr, send_sem, recv_sem, local_sem,
):
    XP, XM = device(0, 1, 0, 0, 0), device(0, 3, 0, 0, 0)
    Y2, YN = device(1, 0, 0, 0, 0), device(0, 0, 1, 0, 0)
    ZP, ZM = device(0, 0, 0, 1, 0), device(0, 0, 0, 3, 0)
    CORE = device(0, 0, 0, 0, 1)
    started = []

    def send(src, dst, to):
        i = len(started)
        copy = pltpu.make_async_remote_copy(
            src_ref=src, dst_ref=dst, send_sem=send_sem.at[i], recv_sem=recv_sem.at[i],
            device_id=to, device_id_type=MESH,
        )
        copy.start()
        started.append(copy)
        return copy

    tok_loads = []
    for s in range(SHARDS):
        load = pltpu.make_async_copy(tok_hbm.at[:, shard_columns(s)], c1r.at[s, pl.ds(0, RUN)], local_sem.at[s])
        load.start()
        tok_loads.append(load)
    own_loads = []
    for k, (src, dst) in enumerate(((wg_hbm, wg), (wu_hbm, wu), (wd_hbm, wd))):
        load = pltpu.make_async_copy(src, dst.at[0], local_sem.at[8 + k])
        load.start()
        own_loads.append(load)

    barrier = pltpu.get_barrier_semaphore()
    for to in (XP, XM, Y2, YN, ZP, ZM, CORE):
        pl.semaphore_signal(barrier, inc=1, device_id=to, device_id_type=MESH)
    pl.semaphore_wait(barrier, 7)

    g_x = (send(wg_hbm, wg.at[3], XP), send(wg_hbm, wg.at[1], XM))
    u_x = (send(wu_hbm, wu.at[3], XP), send(wu_hbm, wu.at[1], XM))

    g_y = send(wg_hbm.at[pl.ds(0, 384)], wg.at[4, pl.ds(0, 384)], Y2)

    row = lax.broadcasted_iota(jnp.int32, (SLOTS, RUN), 0)
    picker_t = jnp.where(row == slot_row(ids_ref, slots_ref), 1.0, 0.0).astype(BF16)
    for s in range(SHARDS):
        tok_loads[s].wait()
        xbuf[s, pl.ds(0, SLOTS), :] = jnp.dot(
            picker_t, c1r[s, pl.ds(0, RUN), :], preferred_element_type=F32
        ).astype(BF16)

    def block(rc, ryl, rz, half=None):
        at = pl.ds(rc * 512 + ryl * 256 + rz * 64, 64)
        if half is None:
            return xbuf.at[:, at]
        return xbuf.at[pl.ds(half * 4, 4), at]

    to_core = []

    def core(ryl, rz, half=None):
        to_core.append(send(block(0, ryl, rz, half), block(1, ryl, rz, half), CORE))

    x_y = send(block(0, 0, 0), block(0, 1, 0), YN)
    x_z = (send(block(0, 0, 0), block(0, 0, 3), ZP), send(block(0, 0, 0), block(0, 0, 1), ZM))
    core(0, 0)
    g_y = (g_y, send(wg_hbm.at[pl.ds(384, 384)], wg.at[4, pl.ds(384, 384)], Y2))
    u_y = (send(wu_hbm, wu.at[4], Y2),)

    lo, hi = pl.ds(0, 384), pl.ds(384, 384)
    ring, rest = pl.ds(0, SPLIT), pl.ds(SPLIT, DEPTH - SPLIT)
    ring_lo, ring_hi = pl.ds(0, 272), pl.ds(272, SPLIT - 272)

    def relay_own(w, first):
        first[0].wait_recv()
        a = send(w.at[3, lo], w.at[2, lo], XP)
        first[1].wait_recv()
        b = send(w.at[1, hi], w.at[2, hi], XM)
        c = send(w.at[3, rest], w.at[7, rest], Y2)
        d = send(w.at[1, rest], w.at[5, rest], Y2)
        return a, b, c, d

    def ring_partner(w, first):
        for copy in first:
            copy.wait_recv()
        return send(w.at[4, ring], w.at[7, ring], XP), send(w.at[4, ring], w.at[5, ring], XM)

    def relay_partner(w, first):
        first[0].wait_recv()
        a = send(w.at[7, ring_lo], w.at[6, ring_lo], XP)
        first[1].wait_recv()
        return a, send(w.at[5, ring_hi], w.at[6, ring_hi], XM)

    g_r = relay_own(wg, g_x)
    x_z[0].wait_recv()
    x_zr = [send(block(0, 0, 3, 0), block(0, 0, 2, 0), ZP)]
    core(0, 3)
    x_z[1].wait_recv()
    x_zr.append(send(block(0, 0, 1, 1), block(0, 0, 2, 1), ZM))
    core(0, 1)
    x_y.wait_recv()
    x_yz = (send(block(0, 1, 0), block(0, 1, 3), ZP), send(block(0, 1, 0), block(0, 1, 1), ZM))
    core(1, 0)
    g_p = ring_partner(wg, g_y)
    for half in (0, 1):
        x_zr[half].wait_recv()
        core(0, 2, half)
    u_r = relay_own(wu, u_x)
    x_yz[0].wait_recv()
    x_yzr = [send(block(0, 1, 3, 0), block(0, 1, 2, 0), ZP)]
    core(1, 3)
    x_yz[1].wait_recv()
    x_yzr.append(send(block(0, 1, 1, 1), block(0, 1, 2, 1), ZM))
    core(1, 1)

    def far_rest(w, relays):
        relays[0].wait_recv()
        relays[1].wait_recv()
        return send(w.at[2, rest], w.at[6, rest], Y2)

    g_f = far_rest(wg, g_r)
    u_p = ring_partner(wu, u_y)
    for half in (0, 1):
        x_yzr[half].wait_recv()
        core(1, 2, half)
    u_f = far_rest(wu, u_r)
    d_y = send(wd_hbm, wd.at[4], Y2)
    for copy in to_core:
        copy.wait_recv()

    def gemm(acc, w, s, first=False):
        @pl.loop(0, 2)
        def _(m):
            rows = pl.ds(pl.multiple_of(m * 512, 512), 512)
            part = jnp.dot(xbuf[s, rows, :], w[s], preferred_element_type=F32)
            if first:
                acc[rows, :] = part
            else:
                acc[rows, :] += part

    own_loads[0].wait()
    own_loads[1].wait()
    gemm(accg, wg, 0, True)
    gemm(accu, wu, 0, True)
    gemm(accg, wg, 1)
    gemm(accg, wg, 3)
    gemm(accg, wg, 4)
    gemm(accg, wg, 2)
    g_pr = relay_partner(wg, g_p)
    gemm(accu, wu, 1)
    gemm(accu, wu, 3)
    gemm(accu, wu, 4)
    gemm(accu, wu, 2)
    u_pr = relay_partner(wu, u_p)
    d_x = (send(wd_hbm, wd.at[3], XP), send(wd_hbm, wd.at[1], XM))
    d_y.wait_recv()
    d_p = (send(wd.at[4], wd.at[7], XP), send(wd.at[4], wd.at[5], XM))
    g_r[2].wait_recv()
    gemm(accg, wg, 7)
    g_r[3].wait_recv()
    gemm(accg, wg, 5)
    u_r[2].wait_recv()
    gemm(accu, wu, 7)
    u_r[3].wait_recv()
    gemm(accu, wu, 5)
    for copy in (g_f, *g_pr):
        copy.wait_recv()
    gemm(accg, wg, 6)
    for copy in (u_f, *u_pr):
        copy.wait_recv()
    gemm(accu, wu, 6)

    @pl.loop(0, 4)
    def _(m):
        rows = pl.ds(pl.multiple_of(m * 256, 256), 256)
        gate = accg[rows, :]
        hid[rows, :] = (gate / (1.0 + jnp.exp(-gate)) * accu[rows, :]).astype(BF16)

    for copy in (x_y, *x_z, *x_zr, *x_yz, *x_yzr, *to_core):
        copy.wait_send()

    d_lo, d_hi = pl.ds(0, 256), pl.ds(256, 256)
    c1, z2, z1, y1, outs = {}, {}, {}, {}, {}
    d_r, d_pr = [], []

    def down_ready(s):
        if s == 0:
            own_loads[2].wait()
        elif s == 1:
            d_x[0].wait_recv()
            d_x[1].wait_recv()
            d_r.append(send(wd.at[3, d_lo], wd.at[2, d_lo], XP))
            d_r.append(send(wd.at[1, d_hi], wd.at[2, d_hi], XM))
        elif s == 5:
            d_p[0].wait_recv()
            d_p[1].wait_recv()
            d_pr.append(send(wd.at[7, d_lo], wd.at[6, d_lo], XP))
            d_pr.append(send(wd.at[5, d_hi], wd.at[6, d_hi], XM))
        elif s == 2:
            for copy in d_r:
                copy.wait_recv()
        elif s == 6:
            for copy in d_pr:
                copy.wait_recv()

    def step_core(s):
        down_ready(s)

        @pl.loop(0, 2)
        def _(m):
            rows = pl.ds(pl.multiple_of(512 + m * 256, 256), 256)
            xbuf[s, rows, :] = jnp.dot(hid[rows, :], wd[s], preferred_element_type=F32).astype(BF16)

        c1[s] = send(xbuf.at[s, pl.ds(512, 512)], c1r.at[s], CORE)

    def step_far(i, s):
        c1[s].wait_recv()

        @pl.loop(0, 2)
        def _(m):
            rows = pl.ds(pl.multiple_of(m * 256, 256), 256)
            at = pl.ds(pl.multiple_of(m * 64, 64), 64)
            part = jnp.dot(hid[rows, :], wd[s], preferred_element_type=F32) + c1r[s, rows, :].astype(F32)
            q[i % 3, 0, at, :] = part[0:64]
            q[i % 3, 1, at, :] = part[64:128]
            q[i % 3, 2, at, :] = part[192:256]
            xbuf[s, pl.ds(pl.multiple_of(256 + m * 64, 64), 64), :] = part[128:192].astype(BF16)

        z2[s] = (
            send(xbuf.at[s, pl.ds(256, 128), lo], z2r.at[s, 0], ZP),
            send(xbuf.at[s, pl.ds(256, 128), hi], z2r.at[s, 1], ZM),
        )

    def step_near(i, s):
        z2[s][0].wait_recv()
        z2[s][1].wait_recv()
        xbuf[s, 0:128, 0:384] = (q[i % 3, 1, :, 0:384] + z2r[s, 0].astype(F32)).astype(BF16)
        xbuf[s, 0:128, 384:768] = q[i % 3, 1, :, 384:768].astype(BF16)
        xbuf[s, 128:256, 0:384] = q[i % 3, 2, :, 0:384].astype(BF16)
        xbuf[s, 128:256, 384:768] = (q[i % 3, 2, :, 384:768] + z2r[s, 1].astype(F32)).astype(BF16)
        z1[s] = (
            send(xbuf.at[s, pl.ds(0, 128)], z1r.at[s, 0], ZP),
            send(xbuf.at[s, pl.ds(128, 128)], z1r.at[s, 1], ZM),
        )

    def step_y(i, s):
        z1[s][0].wait_recv()
        z1[s][1].wait_recv()
        total = q[i % 3, 0] + z1r[s, 0].astype(F32) + z1r[s, 1].astype(F32)
        f0[i] = total[0:64]
        xbuf[s, 384:448, :] = total[64:128].astype(BF16)
        y1[s] = send(xbuf.at[s, pl.ds(384, 64)], yr.at[s], YN)

    def step_out(i, s):
        y1[s].wait_recv()
        f0[i] += yr[s].astype(F32)
        outs[i] = pltpu.make_async_copy(f0.at[i], out_hbm.at[:, shard_columns(s)], local_sem.at[11 + i])
        outs[i].start()

    for i in range(SHARDS + 4):
        if i < SHARDS:
            step_core(ORDER[i])
        if 0 <= i - 1 < SHARDS:
            step_far(i - 1, ORDER[i - 1])
        if 0 <= i - 2 < SHARDS:
            step_near(i - 2, ORDER[i - 2])
        if 0 <= i - 3 < SHARDS:
            step_y(i - 3, ORDER[i - 3])
        if 0 <= i - 4 < SHARDS:
            step_out(i - 4, ORDER[i - 4])

    for copy in outs.values():
        copy.wait()
    waited = (x_y, *x_z, *x_zr, *x_yz, *x_yzr, *to_core)
    for copy in started:
        if not any(copy is other for other in waited):
            copy.wait_send()


def body(tokens, expert_ids, slot_ids, gate_probs, gate_weight, up_weight, down_weight):
    hbm, vmem = pl.BlockSpec(memory_space=pl.ANY), pl.BlockSpec(memory_space=pltpu.VMEM)
    ids, slots, probs = expert_ids.T, slot_ids.T, gate_probs.T
    rows = pl.pallas_call(
        kernel,
        out_shape=jax.ShapeDtypeStruct((SLOTS, tokens.shape[1]), F32),
        in_specs=[hbm, vmem, vmem, hbm, hbm, hbm],
        out_specs=hbm,
        scratch_shapes=[
            pltpu.VMEM((SHARDS, ROWS, DEPTH), BF16),
            pltpu.VMEM((SHARDS, DEPTH, UNITS), BF16),
            pltpu.VMEM((SHARDS, DEPTH, UNITS), BF16),
            pltpu.VMEM((SHARDS, UNITS, DEPTH), BF16),
            pltpu.VMEM((ROWS, UNITS), F32),
            pltpu.VMEM((ROWS, UNITS), F32),
            pltpu.VMEM((ROWS, UNITS), BF16),
            pltpu.VMEM((SHARDS, 512, DEPTH), BF16),
            pltpu.VMEM((SHARDS, 2, 128, 384), BF16),
            pltpu.VMEM((SHARDS, 2, 128, DEPTH), BF16),
            pltpu.VMEM((3, 3, 128, DEPTH), F32),
            pltpu.VMEM((SHARDS, SLOTS, DEPTH), F32),
            pltpu.VMEM((SHARDS, SLOTS, DEPTH), BF16),
            pltpu.SemaphoreType.DMA((COPIES,)),
            pltpu.SemaphoreType.DMA((COPIES,)),
            pltpu.SemaphoreType.DMA((20,)),
        ],
        compiler_params=pltpu.CompilerParams(
            collective_id=0, has_side_effects=True, vmem_limit_bytes=62 << 20
        ),
        cost_estimate=pl.CostEstimate(flops=20_000_000_000, bytes_accessed=60_000_000, transcendentals=1_000_000),
    )(tokens, ids, slots, gate_weight, up_weight, down_weight)
    whole = pl.BlockSpec((2, RUN), lambda i: (0, 0))
    return pl.pallas_call(
        combine,
        grid=(4,),
        out_shape=jax.ShapeDtypeStruct(tokens.shape, BF16),
        in_specs=[whole, whole, whole, pl.BlockSpec((SLOTS, 2 * DEPTH), lambda i: (0, i))],
        out_specs=pl.BlockSpec((RUN, 2 * DEPTH), lambda i: (0, i)),
    )(ids, slots, probs, rows)


def solution(mesh):
    return jax.shard_map(
        body,
        mesh=mesh,
        in_specs=(
            P(("dp", "tensor"), None),
            P(("dp", "tensor"), None),
            P(("dp", "tensor"), None),
            P(("dp", "tensor"), None),
            P("dp", "tensor"),
            P("dp", "tensor"),
            P("tensor", "dp"),
        ),
        out_specs=P(("dp", "tensor"), None),
        check_vma=False,
    )
```

```python
import functools

import jax
import jax.numpy as jnp
from jax import lax
from jax.experimental import pallas as pl
from jax.experimental.pallas import tpu as pltpu
from jax.sharding import PartitionSpec as P

MESH = pl.DeviceIdType.MESH
F32 = jnp.float32
BF16 = jnp.bfloat16

SLOTS = 64
RUN = 256
DEPTH = 768
UNITS = 512
ROWS = 1024
SHARDS = 8
COPIES = 144
CORE_SENDS = 16


def place():
    dp, tensor = lax.axis_index("dp"), lax.axis_index("tensor")
    return dp // 4, dp % 4, tensor // 8, (tensor // 2) % 4, tensor % 2


def device(d_yh, d_x, d_yl, d_z, d_c):
    yh, x, yl, z, c = place()
    yh, x, yl, z, c = (yh + d_yh) % 2, (x + d_x) % 4, (yl + d_yl) % 2, (z + d_z) % 4, (c + d_c) % 2
    return (yh * 4 + x, yl * 8 + z * 2 + c)


def shard_columns(s):
    yh, x, _, _, _ = place()
    owner = ((yh + s // 4) % 2) * 4 + (x + s % 4) % 4
    return pl.ds(pl.multiple_of(owner * DEPTH, DEPTH), DEPTH)


def slot_row(ids_ref, slots_ref):
    first = jnp.where(ids_ref[0:1, :] == 0, slots_ref[0:1, :], SLOTS)
    return jnp.minimum(first, jnp.where(ids_ref[1:2, :] == 0, slots_ref[1:2, :], SLOTS))


def combine(ids_ref, slots_ref, probs_ref, rows_ref, mixed_ref):
    row = lax.broadcasted_iota(jnp.int32, (2 * SLOTS, RUN), 0)
    row = jnp.where(row >= SLOTS, row - SLOTS, row)
    picked = row == slot_row(ids_ref, slots_ref)
    weight = jnp.where(ids_ref[0:1, :] == 0, probs_ref[0:1, :], 0.0)
    weight += jnp.where(ids_ref[1:2, :] == 0, probs_ref[1:2, :], 0.0)
    picker = jnp.where(picked, 1.0, 0.0).T.astype(BF16)
    weight = jnp.sum(jnp.where(picked, weight, 0.0).T[:, :SLOTS], axis=1, keepdims=True)
    rows = rows_ref[...]
    head = rows.astype(BF16)
    tail = (rows - head.astype(F32)).astype(BF16)
    both = jnp.concatenate([head, tail], axis=0)
    mixed_ref[...] = (weight * jnp.dot(picker, both, preferred_element_type=F32)).astype(BF16)


def kernel(
    tok_hbm, ids_ref, slots_ref, wg_hbm, wu_hbm, wd_hbm, out_hbm,
    xbuf, other, wgu, wd, acc, ps, pr, hid, c1s, c1r, z2s, z2r, z1s, z1r, q0, f0, ys, yr,
    send_sem, recv_sem, local_sem,
):
    XP, XM = device(0, 1, 0, 0, 0), device(0, 3, 0, 0, 0)
    Y2, YN = device(1, 0, 0, 0, 0), device(0, 0, 1, 0, 0)
    ZP, ZM = device(0, 0, 0, 1, 0), device(0, 0, 0, 3, 0)
    CORE = device(0, 0, 0, 0, 1)
    started = []
    left = []

    def send(src, dst, to):
        i = len(started)
        copy = pltpu.make_async_remote_copy(
            src_ref=src, dst_ref=dst, send_sem=send_sem.at[i], recv_sem=recv_sem.at[i],
            device_id=to, device_id_type=MESH,
        )
        copy.start()
        started.append(copy)
        left.append(copy)
        return copy

    def sent(copy):
        copy.wait_send()
        left[:] = [other_copy for other_copy in left if other_copy is not copy]

    tok_loads = {}
    for s in (4, 5, 6, 7, 0, 1, 2, 3):
        load = pltpu.make_async_copy(tok_hbm.at[:, shard_columns(s)], c1r.at[s, pl.ds(0, RUN)], local_sem.at[s])
        load.start()
        tok_loads[s] = load
    own_loads = []
    for k, (src, dst) in enumerate(((wg_hbm, wgu.at[0, 0]), (wu_hbm, wgu.at[1, 0]), (wd_hbm, wd.at[0]))):
        load = pltpu.make_async_copy(src, dst, local_sem.at[8 + k])
        load.start()
        own_loads.append(load)

    barrier = pltpu.get_barrier_semaphore()
    for to in (XP, XM, Y2, YN, ZP, ZM, CORE):
        pl.semaphore_signal(barrier, inc=1, device_id=to, device_id_type=MESH)
    pl.semaphore_wait(barrier, 7)

    g_x = (send(wg_hbm, wgu.at[0, 3], XP), send(wg_hbm, wgu.at[0, 1], XM))
    u_x = (send(wu_hbm, wgu.at[1, 3], XP), send(wu_hbm, wgu.at[1, 1], XM))

    row = lax.broadcasted_iota(jnp.int32, (SLOTS, RUN), 0)
    picker_t = jnp.where(row == slot_row(ids_ref, slots_ref), 1.0, 0.0).astype(BF16)

    def pack(s):
        tok_loads[s].wait()
        return jnp.dot(picker_t, c1r[s, pl.ds(0, RUN), :], preferred_element_type=F32).astype(BF16)

    def block(w, rc, ryl, rz, half=None):
        at = pl.ds(w * ROWS + rz * 256 + rc * 128 + ryl * 64, 64)
        if half is None:
            return xbuf.at[:, at]
        return xbuf.at[pl.ds(half * 2, 2), at]

    to_core = []

    def core(w, ryl, rz, half=None):
        to_core.append(send(block(w, 0, ryl, rz, half), block(w, 1, ryl, rz, half), CORE))

    def spread(w, ryl):
        return (
            send(block(w, 0, ryl, 0), block(w, 0, ryl, 3), ZP),
            send(block(w, 0, ryl, 0), block(w, 0, ryl, 1), ZM),
        )

    def relay(w, ryl, first):
        first[0].wait_recv()
        up = send(block(w, 0, ryl, 3, 0), block(w, 0, ryl, 2, 0), ZP)
        first[1].wait_recv()
        down = send(block(w, 0, ryl, 1, 1), block(w, 0, ryl, 2, 1), ZM)
        core(w, ryl, 3)
        core(w, ryl, 1)
        return up, down

    def land(w, ryl, relays):
        for half in (0, 1):
            relays[half].wait_recv()
            core(w, ryl, 2, half)

    for r in range(4):
        other[r] = pack(4 + r)
    x_2 = send(other, block(1, 0, 0, 0), Y2)
    for r in range(4):
        xbuf[r, pl.ds(0, SLOTS), :] = pack(r)
    x_z0 = spread(0, 0)
    x_y0 = send(block(0, 0, 0, 0), block(0, 0, 1, 0), YN)
    core(0, 0, 0)

    def relay_weight(k, first):
        first[0].wait_recv()
        a = send(wgu.at[k, 3, pl.ds(0, 384)], wgu.at[k, 2, pl.ds(0, 384)], XP)
        first[1].wait_recv()
        return a, send(wgu.at[k, 1, pl.ds(384, 384)], wgu.at[k, 2, pl.ds(384, 384)], XM)

    x_2.wait_recv()
    x_z1 = spread(1, 0)
    x_y1 = send(block(1, 0, 0, 0), block(1, 0, 1, 0), YN)
    d_y = send(wd_hbm, wd.at[4], Y2)
    core(1, 0, 0)
    x_r0 = relay(0, 0, x_z0)
    x_y0.wait_recv()
    x_yz0 = spread(0, 1)
    core(0, 1, 0)
    g_r = relay_weight(0, g_x)
    x_r1 = relay(1, 0, x_z1)
    x_y1.wait_recv()
    x_yz1 = spread(1, 1)
    core(1, 1, 0)
    land(0, 0, x_r0)
    x_yr0 = relay(0, 1, x_yz0)
    land(1, 0, x_r1)
    u_r = relay_weight(1, u_x)
    d_x = (send(wd_hbm, wd.at[3], XP), send(wd_hbm, wd.at[1], XM))
    x_yr1 = relay(1, 1, x_yz1)
    d_y.wait_recv()
    d_p = (send(wd.at[4], wd.at[7], XP), send(wd.at[4], wd.at[5], XM))
    land(0, 1, x_yr0)
    land(1, 1, x_yr1)
    for copy in to_core:
        copy.wait_recv()
    for load in own_loads:
        load.wait()
    for copy in (*g_r, *u_r):
        copy.wait_recv()

    def partial(w, rz, dst, rows):
        @pl.loop(0, 4)
        def _(n):
            k, columns = n // 2, pl.ds(pl.multiple_of((n % 2) * 256, 256), 256)
            total = jnp.dot(xbuf[0, pl.ds(w * ROWS + rz * 256, 256), :], wgu[k, 0, :, columns], preferred_element_type=F32)
            for r in range(1, 4):
                total += jnp.dot(
                    xbuf[r, pl.ds(w * ROWS + rz * 256, 256), :], wgu[k, r, :, columns], preferred_element_type=F32
                )
            dst[rows, pl.ds(pl.multiple_of(n * 256, 256), 256)] = total.astype(dst.dtype)

    p = {}

    def partial_out(rz):
        partial(1, rz, ps.at[rz], pl.ds(0, 256))
        for rc in (1, 0):
            at = pl.ds(rc * 128, 128)
            p[rz, rc] = send(ps.at[rz, at], pr.at[rz, at], Y2)

    def partial_own(rz):
        partial(0, rz, acc, pl.ds(rz * 256, 256))

    def hidden(rz, rc):
        p[rz, rc].wait_recv()
        rows, at = pl.ds(rz * 256 + rc * 128, 128), pl.ds(rc * 128, 128)
        gate = acc[rows, 0:UNITS] + pr[rz, at, 0:UNITS].astype(F32)
        up = acc[rows, UNITS:] + pr[rz, at, UNITS:].astype(F32)
        hid[rows, :] = (gate / (1.0 + jnp.exp(-gate)) * up).astype(BF16)

    c1, z2, z1, y1, outs = {}, {}, {}, {}, {}
    core_order = []

    def down(rz, rc, s):
        return jnp.dot(hid[pl.ds(rz * 256 + rc * 128, 128), :], wd[s], preferred_element_type=F32)

    def to_sibling(rz, *shards):
        for s in shards:
            i = len(core_order)
            if i >= CORE_SENDS:
                sent(core_order[i - CORE_SENDS])
            c1s[i % CORE_SENDS] = down(rz, 1, s).astype(BF16)
            c1[rz, s] = send(c1s.at[i % CORE_SENDS], c1r.at[s, pl.ds(rz * 128, 128)], CORE)
            core_order.append(c1[rz, s])

    def sums(rz, *shards):
        for s in shards:
            c1[rz, s].wait_recv()
            total = down(rz, 0, s) + c1r[s, pl.ds(rz * 128, 128), :].astype(F32)
            if rz == 0:
                q0[s] = total
            elif rz == 2:
                z2s[s, 0] = total[:, 0:384].astype(BF16)
                z2s[s, 1] = total[:, 384:768].astype(BF16)
                z2[s] = (send(z2s.at[s, 0], z2r.at[s, 0], ZP), send(z2s.at[s, 1], z2r.at[s, 1], ZM))
            elif rz == 1:
                z2[s][0].wait_recv()
                z1s[s, 0, :, 0:384] = (total[:, 0:384] + z2r[s, 0].astype(F32)).astype(BF16)
                z1s[s, 0, :, 384:768] = total[:, 384:768].astype(BF16)
                z1[s, 0] = send(z1s.at[s, 0], z1r.at[s, 0], ZP)
            else:
                z2[s][1].wait_recv()
                z1s[s, 1, :, 0:384] = total[:, 0:384].astype(BF16)
                z1s[s, 1, :, 384:768] = (total[:, 384:768] + z2r[s, 1].astype(F32)).astype(BF16)
                z1[s, 1] = send(z1s.at[s, 1], z1r.at[s, 1], ZM)

    def to_y(*shards):
        for s in shards:
            z1[s, 0].wait_recv()
            z1[s, 1].wait_recv()
            total = q0[s] + z1r[s, 0].astype(F32) + z1r[s, 1].astype(F32)
            f0[s] = total[0:64]
            ys[s] = total[64:128].astype(BF16)
            y1[s] = send(ys.at[s], yr.at[s], YN)

    def rows_out(*shards):
        for s in shards:
            y1[s].wait_recv()
            f0[s] += yr[s].astype(F32)
            outs[s] = pltpu.make_async_copy(f0.at[s], out_hbm.at[:, shard_columns(s)], local_sem.at[11 + s])
            outs[s].start()

    def relay_down(first, near, far, opposite):
        first[0].wait_recv()
        a = send(wd.at[near, pl.ds(0, 256)], wd.at[far, pl.ds(0, 256)], XP)
        first[1].wait_recv()
        return a, send(wd.at[opposite, pl.ds(256, 256)], wd.at[far, pl.ds(256, 256)], XM)

    partial_out(2)
    partial_out(1)
    partial_own(2)
    partial_out(3)
    partial_out(0)
    hidden(2, 1)
    to_sibling(2, 0, 4)
    partial_own(1)
    hidden(2, 0)
    sums(2, 0, 4)
    d_r = relay_down(d_x, 3, 2, 1)
    to_sibling(2, 1, 3)
    sums(2, 1, 3)
    partial_own(3)
    hidden(1, 1)
    to_sibling(1, 0, 4, 1, 3)
    partial_own(0)
    hidden(1, 0)
    sums(1, 0, 4, 1, 3)
    d_pr = relay_down(d_p, 7, 6, 5)
    to_sibling(2, 5, 7)
    sums(2, 5, 7)
    hidden(3, 1)
    to_sibling(3, 0, 4, 1, 3)
    hidden(3, 0)
    sums(3, 0, 4, 1, 3)
    to_sibling(1, 5, 7)
    to_sibling(3, 5, 7)
    sums(1, 5, 7)
    sums(3, 5, 7)
    d_r[0].wait_recv()
    d_r[1].wait_recv()
    to_sibling(2, 2)
    hidden(0, 1)
    sums(2, 2)
    to_sibling(0, 0, 4, 1, 3)
    to_sibling(1, 2)
    to_sibling(3, 2)
    hidden(0, 0)
    sums(1, 2)
    sums(3, 2)
    d_pr[0].wait_recv()
    d_pr[1].wait_recv()
    to_sibling(2, 6)
    sums(0, 0, 4)
    sums(2, 6)
    to_sibling(1, 6)
    to_sibling(3, 6)
    sums(0, 1, 3)
    to_y(0, 4, 1)
    sums(1, 6)
    sums(3, 6)
    to_y(3)
    to_sibling(0, 5, 7, 2, 6)
    sums(0, 5, 7, 2, 6)
    rows_out(0, 4, 1, 3)
    to_y(5, 7)
    to_y(2)
    rows_out(5, 7)
    to_y(6)
    rows_out(2, 6)

    for copy in outs.values():
        copy.wait()
    for copy in list(left):
        copy.wait_send()


def body(tokens, expert_ids, slot_ids, gate_probs, gate_weight, up_weight, down_weight):
    hbm, vmem = pl.BlockSpec(memory_space=pl.ANY), pl.BlockSpec(memory_space=pltpu.VMEM)
    ids, slots, probs = expert_ids.T, slot_ids.T, gate_probs.T
    rows = pl.pallas_call(
        kernel,
        out_shape=jax.ShapeDtypeStruct((SLOTS, tokens.shape[1]), F32),
        in_specs=[hbm, vmem, vmem, hbm, hbm, hbm],
        out_specs=hbm,
        scratch_shapes=[
            pltpu.VMEM((4, 2 * ROWS, DEPTH), BF16),
            pltpu.VMEM((4, SLOTS, DEPTH), BF16),
            pltpu.VMEM((2, 4, DEPTH, UNITS), BF16),
            pltpu.VMEM((SHARDS, UNITS, DEPTH), BF16),
            pltpu.VMEM((ROWS, 2 * UNITS), F32),
            pltpu.VMEM((4, 256, 2 * UNITS), BF16),
            pltpu.VMEM((4, 256, 2 * UNITS), BF16),
            pltpu.VMEM((ROWS, UNITS), BF16),
            pltpu.VMEM((CORE_SENDS, 128, DEPTH), BF16),
            pltpu.VMEM((SHARDS, 512, DEPTH), BF16),
            pltpu.VMEM((SHARDS, 2, 128, 384), BF16),
            pltpu.VMEM((SHARDS, 2, 128, 384), BF16),
            pltpu.VMEM((SHARDS, 2, 128, DEPTH), BF16),
            pltpu.VMEM((SHARDS, 2, 128, DEPTH), BF16),
            pltpu.VMEM((SHARDS, 128, DEPTH), F32),
            pltpu.VMEM((SHARDS, SLOTS, DEPTH), F32),
            pltpu.VMEM((SHARDS, SLOTS, DEPTH), BF16),
            pltpu.VMEM((SHARDS, SLOTS, DEPTH), BF16),
            pltpu.SemaphoreType.DMA((COPIES,)),
            pltpu.SemaphoreType.DMA((COPIES,)),
            pltpu.SemaphoreType.DMA((20,)),
        ],
        compiler_params=pltpu.CompilerParams(
            collective_id=0, has_side_effects=True, vmem_limit_bytes=62 << 20
        ),
        cost_estimate=pl.CostEstimate(flops=20_000_000_000, bytes_accessed=60_000_000, transcendentals=1_000_000),
    )(tokens, ids, slots, gate_weight, up_weight, down_weight)
    whole = pl.BlockSpec((2, RUN), lambda i: (0, 0))
    return pl.pallas_call(
        combine,
        grid=(4,),
        out_shape=jax.ShapeDtypeStruct(tokens.shape, BF16),
        in_specs=[whole, whole, whole, pl.BlockSpec((SLOTS, 2 * DEPTH), lambda i: (0, i))],
        out_specs=pl.BlockSpec((RUN, 2 * DEPTH), lambda i: (0, i)),
    )(ids, slots, probs, rows)


def solution(mesh):
    return jax.shard_map(
        body,
        mesh=mesh,
        in_specs=(
            P(("dp", "tensor"), None),
            P(("dp", "tensor"), None),
            P(("dp", "tensor"), None),
            P(("dp", "tensor"), None),
            P("dp", "tensor"),
            P("dp", "tensor"),
            P("tensor", "dp"),
        ),
        out_specs=P(("dp", "tensor"), None),
        check_vma=False,
    )
```

```python
import functools

import jax
import jax.numpy as jnp
from jax import lax
from jax.experimental import pallas as pl
from jax.experimental.pallas import tpu as pltpu
from jax.sharding import PartitionSpec as P

MESH = pl.DeviceIdType.MESH
F32 = jnp.float32
BF16 = jnp.bfloat16

SLOTS = 64
RUN = 256
DEPTH = 768
UNITS = 512
ROWS = 1024
SHARDS = 8
COPIES = 176
KEPT = 16

ORDER = (0, 4, 1, 3, 5, 7, 2, 6)
Y_FIRST = 7


def place():
    dp, tensor = lax.axis_index("dp"), lax.axis_index("tensor")
    return dp // 4, dp % 4, tensor // 8, (tensor // 2) % 4, tensor % 2


def device(d_yh, d_x, d_yl, d_z, d_c):
    yh, x, yl, z, c = place()
    yh, x, yl, z, c = (yh + d_yh) % 2, (x + d_x) % 4, (yl + d_yl) % 2, (z + d_z) % 4, (c + d_c) % 2
    return (yh * 4 + x, yl * 8 + z * 2 + c)


def shard_columns(s):
    yh, x, _, _, _ = place()
    owner = ((yh + s // 4) % 2) * 4 + (x + s % 4) % 4
    return pl.ds(pl.multiple_of(owner * DEPTH, DEPTH), DEPTH)


def slot_row(ids_ref, slots_ref):
    first = jnp.where(ids_ref[0:1, :] == 0, slots_ref[0:1, :], SLOTS)
    return jnp.minimum(first, jnp.where(ids_ref[1:2, :] == 0, slots_ref[1:2, :], SLOTS))


def combine(picker_ref, weight_ref, rows_ref, mixed_ref):
    mixed = jnp.dot(picker_ref[...], rows_ref[...], preferred_element_type=F32)
    mixed_ref[...] = (weight_ref[:, 0:1] * mixed).astype(BF16)


def kernel(
    tok_hbm, ids_ref, slots_ref, probs_ref, wg_hbm, wu_hbm, wd_hbm, out_hbm, picker_ref, weight_ref,
    xbuf, other, wgu, wd, acc, ps, pr, hid, c1s, keep, c1r, z2s, z2r, z1s, z1r, q0, ys, yr,
    send_sem, recv_sem, local_sem,
):
    XP, XM = device(0, 1, 0, 0, 0), device(0, 3, 0, 0, 0)
    Y2, YN = device(1, 0, 0, 0, 0), device(0, 0, 1, 0, 0)
    ZP, ZM = device(0, 0, 0, 1, 0), device(0, 0, 0, 3, 0)
    CORE = device(0, 0, 0, 0, 1)
    started, left, here = [], {}, set()

    def send(src, dst, to):
        i = len(started)
        copy = pltpu.make_async_remote_copy(
            src_ref=src, dst_ref=dst, send_sem=send_sem.at[i], recv_sem=recv_sem.at[i],
            device_id=to, device_id_type=MESH,
        )
        copy.start()
        started.append(copy)
        left[i] = copy
        return i

    def arrived(*copies):
        for i in copies:
            if i not in here:
                started[i].wait_recv()
                here.add(i)

    def sent(i):
        if i in left:
            left.pop(i).wait_send()

    tok_loads = {}
    for s in (4, 5, 6, 7, 0, 1, 2, 3):
        load = pltpu.make_async_copy(tok_hbm.at[:, shard_columns(s)], c1r.at[s, pl.ds(0, RUN)], local_sem.at[s])
        load.start()
        tok_loads[s] = load
    own_loads = []
    half = (pl.ds(0, 256), pl.ds(256, 256))
    for h in (0, 1):
        for k, src in enumerate((wg_hbm, wu_hbm)):
            own_loads.append(
                pltpu.make_async_copy(src.at[:, half[h]], wgu.at[h, 0, :, half[k]], local_sem.at[8 + 2 * h + k])
            )
    own_loads.append(pltpu.make_async_copy(wd_hbm, wd.at[0], local_sem.at[12]))
    for load in own_loads:
        load.start()

    barrier = pltpu.get_barrier_semaphore()
    for to in (XP, XM, Y2, YN, ZP, ZM, CORE):
        pl.semaphore_signal(barrier, inc=1, device_id=to, device_id_type=MESH)
    pl.semaphore_wait(barrier, 7)

    w_x = {}
    for h in (0, 1):
        for k, src in enumerate((wg_hbm, wu_hbm)):
            w_x[h, k] = (
                send(src.at[:, half[h]], wgu.at[h, 3, :, half[k]], XP),
                send(src.at[:, half[h]], wgu.at[h, 1, :, half[k]], XM),
            )

    row = lax.broadcasted_iota(jnp.int32, (SLOTS, RUN), 0)
    picker_t = jnp.where(row == slot_row(ids_ref, slots_ref), 1.0, 0.0).astype(BF16)

    def pack(s):
        tok_loads[s].wait()
        return jnp.dot(picker_t, c1r[s, pl.ds(0, RUN), :], preferred_element_type=F32).astype(BF16)

    def block(w, rc, ryl, rz, part=None):
        at = pl.ds(w * ROWS + rz * 256 + ryl * 128 + rc * 64, 64)
        if part is None:
            return xbuf.at[:, at]
        return xbuf.at[pl.ds(part * 2, 2), at]

    from_core = {}

    def core(w, ryl, rz, part=None):
        copy = send(block(w, 0, ryl, rz, part), block(w, 1, ryl, rz, part), CORE)
        from_core.setdefault((w, rz), []).append(copy)

    def spread(w, ryl):
        return (
            send(block(w, 0, ryl, 0), block(w, 0, ryl, 3), ZP),
            send(block(w, 0, ryl, 0), block(w, 0, ryl, 1), ZM),
        )

    def relay(w, ryl, first):
        arrived(first[0])
        up = send(block(w, 0, ryl, 3, 0), block(w, 0, ryl, 2, 0), ZP)
        arrived(first[1])
        return up, send(block(w, 0, ryl, 1, 1), block(w, 0, ryl, 2, 1), ZM)

    def both_cores(w, ryl, first):
        arrived(*first)
        core(w, ryl, 3)
        core(w, ryl, 1)

    def land(w, ryl, relays):
        for part in (0, 1):
            arrived(relays[part])
            core(w, ryl, 2, part)

    for r in range(4):
        other[r] = pack(4 + r)
    x_2 = send(other, block(1, 0, 0, 0), Y2)
    for r in range(4):
        xbuf[r, pl.ds(0, SLOTS), :] = pack(r)
    x_z0 = spread(0, 0)
    x_y0 = send(block(0, 0, 0, 0), block(0, 0, 1, 0), YN)
    core(0, 0, 0)

    upper, lower = pl.ds(0, 384), pl.ds(384, 384)

    def relay_weight(h):
        copies = []
        for k in (0, 1):
            arrived(w_x[h, k][0])
            copies.append(send(wgu.at[h, 3, upper, half[k]], wgu.at[h, 2, upper, half[k]], XP))
            arrived(w_x[h, k][1])
            copies.append(send(wgu.at[h, 1, lower, half[k]], wgu.at[h, 2, lower, half[k]], XM))
        return copies

    def partial(w, rz, h, dst, rows, shards=(0, 1, 3, 2), more=False):
        arrived(*from_core[w, rz])
        if 2 in shards:
            arrived(*(w_r0, w_r1)[h])

        @pl.loop(0, 2)
        def _(n):
            columns = pl.ds(pl.multiple_of(n * 256, 256), 256)
            at = pl.ds(w * ROWS + rz * 256, 256)
            into = pl.ds(pl.multiple_of(h * 512 + n * 256, 256), 256)
            total = dst[rows, into] if more else None
            for r in shards:
                part = jnp.dot(xbuf[r, at, :], wgu[h, r, :, columns], preferred_element_type=F32)
                total = part if total is None else total + part
            dst[rows, into] = total.astype(dst.dtype)

    def partial_out(rz, h):
        partial(1, rz, h, ps.at[rz], pl.ds(0, 256))

    def partial_own(rz, **kind):
        for h in (0, 1):
            partial(0, rz, h, acc, pl.ds(rz * 256, 256), **kind)

    def partial_last(rz):
        partial_own(rz, shards=(2,), more=True)

    row = lax.broadcasted_iota(jnp.int32, (2 * SLOTS, RUN), 0)
    picked = jnp.where(row >= SLOTS, row - SLOTS, row) == slot_row(ids_ref, slots_ref)
    weight = jnp.where(ids_ref[0:1, :] == 0, probs_ref[0:1, :], 0.0)
    weight += jnp.where(ids_ref[1:2, :] == 0, probs_ref[1:2, :], 0.0)
    picker_ref[...] = jnp.where(picked, 1.0, 0.0).T.astype(BF16)
    weight = jnp.sum(jnp.where(picked, weight, 0.0).T[:, :SLOTS], axis=1, keepdims=True)
    weight_ref[...] = jnp.broadcast_to(weight, (RUN, 2 * SLOTS))

    arrived(x_2)
    x_z1 = spread(1, 0)
    x_y1 = send(block(1, 0, 0, 0), block(1, 0, 1, 0), YN)
    d_y = send(wd_hbm, wd.at[4], Y2)
    core(1, 0, 0)
    both_cores(0, 0, x_z0)
    arrived(x_y0)
    x_yz0 = spread(0, 1)
    core(0, 1, 0)
    x_r1 = relay(1, 0, x_z1)
    both_cores(1, 0, x_z1)
    w_r0 = relay_weight(0)
    arrived(x_y1)
    x_yz1 = spread(1, 1)
    core(1, 1, 0)
    both_cores(0, 1, x_yz0)
    land(1, 0, x_r1)
    w_r1 = relay_weight(1)
    d_x = (send(wd_hbm, wd.at[3], XP), send(wd_hbm, wd.at[1], XM))
    for load in own_loads:
        load.wait()
    partial_own(0, shards=(0, 1, 3))
    partial_own(1, shards=(0, 1, 3))
    partial_own(3, shards=(0, 1, 3))
    x_yr1 = relay(1, 1, x_yz1)
    x_r0 = relay(0, 0, x_z0)
    x_yr0 = relay(0, 1, x_yz0)
    both_cores(1, 1, x_yz1)
    arrived(d_y)
    d_p = (send(wd.at[4], wd.at[7], XP), send(wd.at[4], wd.at[5], XM))
    partial_out(0, 0)
    land(1, 1, x_yr1)
    partial_out(1, 0)

    p = {(rz, ryl): [] for rz in range(4) for ryl in (0, 1)}

    def exchange(rz, ryl):
        at = pl.ds(ryl * 128, 128)
        p[rz, ryl].append(send(ps.at[rz, at], pr.at[rz, at], Y2))

    def hidden(rz, ryl):
        arrived(*p[rz, ryl])
        rows, at = pl.ds(rz * 256 + ryl * 128, 128), pl.ds(ryl * 128, 128)
        for h in (0, 1):
            g, u = pl.ds(h * 512, 256), pl.ds(h * 512 + 256, 256)
            gate = acc[rows, g] + pr[rz, at, g].astype(F32)
            up = acc[rows, u] + pr[rz, at, u].astype(F32)
            hid[rows, half[h]] = (gate / (1.0 + jnp.exp(-gate)) * up).astype(BF16)

    c1, z2, z1, y1, outs = {}, {}, {}, {}, {}
    slots, busy = [], set()

    def down(rz, ryl, first, count):
        if len(slots) % KEPT + count > KEPT:
            slots.extend([None] * (KEPT - len(slots) % KEPT))
        start = len(slots) % KEPT
        for j in range(count):
            if len(slots) + j >= KEPT and slots[len(slots) + j - KEPT] is not None:
                sent(slots[len(slots) + j - KEPT])
        assert busy.isdisjoint(range(start, start + count))
        busy.update(range(start, start + count))
        rows = pl.ds(rz * 256 + ryl * 128, 128)
        for j in range(count):
            part = jnp.dot(hid[rows, :], wd[ORDER[first + j]], preferred_element_type=F32)
            keep[start + j] = part[0:64]
            c1s[pl.ds((start + j) * 64, 64), :] = part[64:128].astype(BF16)
        copy = send(
            c1s.at[pl.ds(start * 64, count * 64)], c1r.at[rz * 2 + ryl, pl.ds(first * 64, count * 64)], CORE
        )
        slots.extend([copy] * count)
        c1[rz, ryl, first] = (copy, start, count)

    def sums(rz, ryl, first):
        copy, start, count = c1[rz, ryl, first]
        arrived(copy)
        for j in range(count):
            t = first + j
            total = keep[start + j] + c1r[rz * 2 + ryl, pl.ds(t * 64, 64), :].astype(F32)
            if t >= Y_FIRST:
                spot = Y_FIRST + (t - Y_FIRST) * 4 + rz
                if ryl == 1:
                    ys[spot] = total.astype(BF16)
                    y1[t, rz] = send(ys.at[spot], yr.at[spot], YN)
                    continue
                arrived(y1[t, rz])
                total += yr[spot].astype(F32)
            if rz == 0:
                q0[ryl, t] = total
            elif rz == 2:
                z2s[ryl, 0, t] = total[:, 0:384].astype(BF16)
                z2s[ryl, 1, t] = total[:, 384:768].astype(BF16)
            elif rz == 1:
                arrived(z2[ryl, 0, t])
                z1s[ryl, 0, t, :, 0:384] = (total[:, 0:384] + z2r[ryl, 0, t].astype(F32)).astype(BF16)
                z1s[ryl, 0, t, :, 384:768] = total[:, 384:768].astype(BF16)
            else:
                arrived(z2[ryl, 1, t])
                z1s[ryl, 1, t, :, 0:384] = total[:, 0:384].astype(BF16)
                z1s[ryl, 1, t, :, 384:768] = (total[:, 384:768] + z2r[ryl, 1, t].astype(F32)).astype(BF16)
        busy.difference_update(range(start, start + count))
        if first >= Y_FIRST and ryl == 1:
            return
        group = pl.ds(first, count)
        for way, to in ((0, ZP), (1, ZM)):
            if rz == 2:
                copy = send(z2s.at[ryl, way, group], z2r.at[ryl, way, group], to)
                for j in range(count):
                    z2[ryl, way, first + j] = copy
            elif rz == (1, 3)[way]:
                copy = send(z1s.at[ryl, way, group], z1r.at[ryl, way, group], to)
                for j in range(count):
                    z1[ryl, way, first + j] = copy

    def both(rz, ryl, first, count):
        down(rz, ryl, first, count)
        sums(rz, ryl, first)

    def over_z(ryl, t):
        arrived(z1[ryl, 0, t], z1[ryl, 1, t])
        return q0[ryl, t] + z1r[ryl, 0, t].astype(F32) + z1r[ryl, 1, t].astype(F32)

    def to_y(first, count):
        for t in range(first, first + count):
            ys[t] = over_z(1, t).astype(BF16)
        group = pl.ds(first, count)
        copy = send(ys.at[group], yr.at[group], YN)
        for t in range(first, first + count):
            y1[t] = copy

    def rows_out(first, count):
        for t in range(first, first + count):
            total = over_z(0, t)
            if t < Y_FIRST:
                arrived(y1[t])
                total += yr[t].astype(F32)
            head = total.astype(BF16)
            z1r[0, 0, t] = head
            z1r[0, 1, t] = (total - head.astype(F32)).astype(BF16)
            for part in (0, 1):
                outs[t, part] = pltpu.make_async_copy(
                    z1r.at[0, part, t],
                    out_hbm.at[pl.ds(part * SLOTS, SLOTS), shard_columns(ORDER[t])],
                    local_sem.at[13 + 2 * t + part],
                )
                outs[t, part].start()

    def relay_down(first, near, far, opposite):
        arrived(first[0])
        a = send(wd.at[near, half[0]], wd.at[far, half[0]], XP)
        arrived(first[1])
        return a, send(wd.at[opposite, half[1]], wd.at[far, half[1]], XM)

    partial_out(2, 0)
    early = send(ps.at[2, :, pl.ds(0, 512)], pr.at[2, :, pl.ds(0, 512)], Y2)
    land(0, 0, x_r0)
    land(0, 1, x_yr0)
    partial_out(3, 0)
    partial_out(2, 1)
    for ryl in (1, 0):
        at = pl.ds(ryl * 128, 128), pl.ds(512, 512)
        p[2, ryl] += [early, send(ps.at[2, at[0], at[1]], pr.at[2, at[0], at[1]], Y2)]
    partial_out(1, 1)
    exchange(1, 1)
    partial_out(3, 1)
    exchange(3, 1)
    exchange(1, 0)
    exchange(3, 0)
    partial_own(2)
    hidden(2, 1)
    down(2, 1, 0, 2)
    partial_last(1)
    sums(2, 1, 0)
    hidden(2, 0)
    down(2, 0, 0, 2)
    partial_out(0, 1)
    exchange(0, 1)
    exchange(0, 0)
    sums(2, 0, 0)
    hidden(1, 1)
    down(1, 1, 0, 2)
    d_r = relay_down(d_x, 3, 2, 1)
    down(2, 1, 2, 2)
    down(2, 0, 2, 2)
    sums(1, 1, 0)
    sums(2, 1, 2)
    sums(2, 0, 2)
    down(1, 1, 2, 2)
    partial_last(3)
    sums(1, 1, 2)
    hidden(3, 1)
    down(3, 1, 0, 4)
    partial_last(0)
    sums(3, 1, 0)
    hidden(1, 0)
    down(1, 0, 0, 4)
    sums(1, 0, 0)
    hidden(3, 0)
    down(3, 0, 0, 4)
    d_pr = relay_down(d_p, 7, 6, 5)
    down(2, 1, 4, 2)
    down(2, 0, 4, 2)
    sums(2, 1, 4)
    sums(2, 0, 4)
    sums(3, 0, 0)
    hidden(0, 1)
    down(0, 1, 0, 4)
    down(1, 1, 4, 2)
    down(3, 1, 4, 2)
    sums(0, 1, 0)
    sums(1, 1, 4)
    sums(3, 1, 4)
    down(1, 0, 4, 2)
    down(3, 0, 4, 2)
    to_y(0, 4)
    sums(1, 0, 4)
    sums(3, 0, 4)
    arrived(*d_r)
    down(2, 1, 6, 1)
    down(2, 0, 6, 1)
    hidden(0, 0)
    down(0, 0, 0, 4)
    sums(2, 1, 6)
    sums(2, 0, 6)
    down(0, 1, 4, 2)
    sums(0, 0, 0)
    down(0, 0, 4, 2)
    sums(0, 1, 4)
    sums(0, 0, 4)
    for rz, ryl in ((1, 1), (3, 1), (1, 0), (3, 0), (0, 1), (0, 0)):
        down(rz, ryl, 6, 1)
    sums(0, 1, 6)
    sums(0, 0, 6)
    arrived(*d_pr)
    for rz in (2, 3, 1, 0):
        down(rz, 1, 7, 1)
    for rz in (2, 3, 1, 0):
        sums(rz, 1, 7)
    for rz, ryl in ((1, 1), (3, 1), (1, 0), (3, 0)):
        sums(rz, ryl, 6)
    for rz in (2, 3, 1, 0):
        down(rz, 0, 7, 1)
    sums(2, 0, 7)
    to_y(4, 2)
    sums(3, 0, 7)
    sums(1, 0, 7)
    sums(0, 0, 7)
    rows_out(0, 4)
    to_y(6, 1)
    rows_out(4, 2)
    rows_out(7, 1)
    rows_out(6, 1)

    for copy in outs.values():
        copy.wait()
    for copy in left.values():
        copy.wait_send()
    assert len(started) <= COPIES


def body(tokens, expert_ids, slot_ids, gate_probs, gate_weight, up_weight, down_weight):
    hbm, vmem = pl.BlockSpec(memory_space=pl.ANY), pl.BlockSpec(memory_space=pltpu.VMEM)
    ids, slots, probs = expert_ids.T, slot_ids.T, gate_probs.T
    rows, picker, weight = pl.pallas_call(
        kernel,
        out_shape=(
            jax.ShapeDtypeStruct((2 * SLOTS, tokens.shape[1]), BF16),
            jax.ShapeDtypeStruct((RUN, 2 * SLOTS), BF16),
            jax.ShapeDtypeStruct((RUN, 2 * SLOTS), F32),
        ),
        in_specs=[hbm, vmem, vmem, vmem, hbm, hbm, hbm],
        out_specs=(hbm, vmem, vmem),
        scratch_shapes=[
            pltpu.VMEM((4, 2 * ROWS, DEPTH), BF16),
            pltpu.VMEM((4, SLOTS, DEPTH), BF16),
            pltpu.VMEM((2, 4, DEPTH, UNITS), BF16),
            pltpu.VMEM((SHARDS, UNITS, DEPTH), BF16),
            pltpu.VMEM((ROWS, 2 * UNITS), F32),
            pltpu.VMEM((4, 256, 2 * UNITS), BF16),
            pltpu.VMEM((4, 256, 2 * UNITS), BF16),
            pltpu.VMEM((ROWS, UNITS), BF16),
            pltpu.VMEM((KEPT * 64, DEPTH), BF16),
            pltpu.VMEM((KEPT, 64, DEPTH), F32),
            pltpu.VMEM((8, SHARDS * 64, DEPTH), BF16),
            pltpu.VMEM((2, 2, SHARDS, 64, 384), BF16),
            pltpu.VMEM((2, 2, SHARDS, 64, 384), BF16),
            pltpu.VMEM((2, 2, SHARDS, 64, DEPTH), BF16),
            pltpu.VMEM((2, 2, SHARDS, 64, DEPTH), BF16),
            pltpu.VMEM((2, SHARDS, 64, DEPTH), F32),
            pltpu.VMEM((Y_FIRST + (SHARDS - Y_FIRST) * 4, SLOTS, DEPTH), BF16),
            pltpu.VMEM((Y_FIRST + (SHARDS - Y_FIRST) * 4, SLOTS, DEPTH), BF16),
            pltpu.SemaphoreType.DMA((COPIES,)),
            pltpu.SemaphoreType.DMA((COPIES,)),
            pltpu.SemaphoreType.DMA((29,)),
        ],
        compiler_params=pltpu.CompilerParams(
            collective_id=0, has_side_effects=True, vmem_limit_bytes=62 << 20
        ),
        cost_estimate=pl.CostEstimate(flops=20_000_000_000, bytes_accessed=60_000_000, transcendentals=1_000_000),
    )(tokens, ids, slots, probs, gate_weight, up_weight, down_weight)
    small = pl.BlockSpec((RUN, 2 * SLOTS), lambda i: (0, 0))
    return pl.pallas_call(
        combine,
        grid=(2,),
        out_shape=jax.ShapeDtypeStruct(tokens.shape, BF16),
        in_specs=[small, small, pl.BlockSpec((2 * SLOTS, 4 * DEPTH), lambda i: (0, i))],
        out_specs=pl.BlockSpec((RUN, 4 * DEPTH), lambda i: (0, i)),
    )(picker, weight, rows)


def solution(mesh):
    return jax.shard_map(
        body,
        mesh=mesh,
        in_specs=(
            P(("dp", "tensor"), None),
            P(("dp", "tensor"), None),
            P(("dp", "tensor"), None),
            P(("dp", "tensor"), None),
            P("dp", "tensor"),
            P("dp", "tensor"),
            P("tensor", "dp"),
        ),
        out_specs=P(("dp", "tensor"), None),
        check_vma=False,
    )
```

```python
import functools

import jax
import jax.numpy as jnp
from jax import lax
from jax.experimental import pallas as pl
from jax.experimental.pallas import tpu as pltpu
from jax.sharding import PartitionSpec as P

MESH = pl.DeviceIdType.MESH
F32 = jnp.float32
BF16 = jnp.bfloat16

SLOTS = 64
RUN = 256
DEPTH = 768
UNITS = 512
ROWS = 1024
SHARDS = 8
COPIES = 176
KEPT = 16

ORDER = (0, 4, 1, 3, 5, 7, 2, 6)
Y_FIRST = 7


def place():
    dp, tensor = lax.axis_index("dp"), lax.axis_index("tensor")
    return dp // 4, dp % 4, tensor // 8, (tensor // 2) % 4, tensor % 2


def device(d_yh, d_x, d_yl, d_z, d_c):
    yh, x, yl, z, c = place()
    yh, x, yl, z, c = (yh + d_yh) % 2, (x + d_x) % 4, (yl + d_yl) % 2, (z + d_z) % 4, (c + d_c) % 2
    return (yh * 4 + x, yl * 8 + z * 2 + c)


def shard_columns(s):
    yh, x, _, _, _ = place()
    owner = ((yh + s // 4) % 2) * 4 + (x + s % 4) % 4
    return pl.ds(pl.multiple_of(owner * DEPTH, DEPTH), DEPTH)


def slot_row(ids_ref, slots_ref):
    first = jnp.where(ids_ref[0:1, :] == 0, slots_ref[0:1, :], SLOTS)
    return jnp.minimum(first, jnp.where(ids_ref[1:2, :] == 0, slots_ref[1:2, :], SLOTS))


def combine(picker_ref, weight_ref, rows_ref, mixed_ref):
    mixed = jnp.dot(picker_ref[...], rows_ref[...], preferred_element_type=F32)
    mixed_ref[...] = (weight_ref[:, 0:1] * mixed).astype(BF16)


def kernel(
    tok_hbm, ids_ref, slots_ref, probs_ref, wg_hbm, wu_hbm, wd_hbm, out_hbm, picker_ref, weight_ref,
    xbuf, other, wgu, wd, acc, ps, pr, hid, c1s, keep, c1r, z2s, z2r, z1s, z1r, q0, ys, yr,
    send_sem, recv_sem, local_sem,
):
    XP, XM = device(0, 1, 0, 0, 0), device(0, 3, 0, 0, 0)
    Y2, YN = device(1, 0, 0, 0, 0), device(0, 0, 1, 0, 0)
    ZP, ZM = device(0, 0, 0, 1, 0), device(0, 0, 0, 3, 0)
    CORE = device(0, 0, 0, 0, 1)
    started, left, here = [], {}, set()

    def send(src, dst, to):
        i = len(started)
        copy = pltpu.make_async_remote_copy(
            src_ref=src, dst_ref=dst, send_sem=send_sem.at[i], recv_sem=recv_sem.at[i],
            device_id=to, device_id_type=MESH,
        )
        copy.start()
        started.append(copy)
        left[i] = copy
        return i

    def arrived(*copies):
        for i in copies:
            if i not in here:
                started[i].wait_recv()
                here.add(i)

    def sent(i):
        if i in left:
            left.pop(i).wait_send()

    tok_loads = {}
    for s in (4, 5, 6, 7, 0, 1, 2, 3):
        load = pltpu.make_async_copy(tok_hbm.at[:, shard_columns(s)], c1r.at[s, pl.ds(0, RUN)], local_sem.at[s])
        load.start()
        tok_loads[s] = load
    own_loads = []
    half = (pl.ds(0, 256), pl.ds(256, 256))
    for h in (0, 1):
        for k, src in enumerate((wg_hbm, wu_hbm)):
            own_loads.append(
                pltpu.make_async_copy(src.at[:, half[h]], wgu.at[h, 0, :, half[k]], local_sem.at[8 + 2 * h + k])
            )
    own_loads.append(pltpu.make_async_copy(wd_hbm, wd.at[0], local_sem.at[12]))
    for load in own_loads:
        load.start()

    barrier = pltpu.get_barrier_semaphore()
    for to in (XP, XM, Y2, YN, ZP, ZM, CORE):
        pl.semaphore_signal(barrier, inc=1, device_id=to, device_id_type=MESH)
    pl.semaphore_wait(barrier, 7)

    w_x = {}
    for h in (0, 1):
        for k, src in enumerate((wg_hbm, wu_hbm)):
            w_x[h, k] = (
                send(src.at[:, half[h]], wgu.at[h, 3, :, half[k]], XP),
                send(src.at[:, half[h]], wgu.at[h, 1, :, half[k]], XM),
            )

    row = lax.broadcasted_iota(jnp.int32, (SLOTS, RUN), 0)
    picker_t = jnp.where(row == slot_row(ids_ref, slots_ref), 1.0, 0.0).astype(BF16)

    def pack(s):
        tok_loads[s].wait()
        return jnp.dot(picker_t, c1r[s, pl.ds(0, RUN), :], preferred_element_type=F32).astype(BF16)

    def block(w, rc, ryl, rz, part=None):
        at = pl.ds(w * ROWS + rz * 256 + ryl * 128 + rc * 64, 64)
        if part is None:
            return xbuf.at[:, at]
        return xbuf.at[pl.ds(part * 2, 2), at]

    from_core = {}

    def core(w, ryl, rz, part=None):
        copy = send(block(w, 0, ryl, rz, part), block(w, 1, ryl, rz, part), CORE)
        from_core.setdefault((w, rz), []).append(copy)

    def spread(w, ryl):
        return (
            send(block(w, 0, ryl, 0), block(w, 0, ryl, 3), ZP),
            send(block(w, 0, ryl, 0), block(w, 0, ryl, 1), ZM),
        )

    def relay(w, ryl, first):
        arrived(first[0])
        up = send(block(w, 0, ryl, 3, 0), block(w, 0, ryl, 2, 0), ZP)
        arrived(first[1])
        return up, send(block(w, 0, ryl, 1, 1), block(w, 0, ryl, 2, 1), ZM)

    def both_cores(w, ryl, first):
        arrived(*first)
        core(w, ryl, 3)
        core(w, ryl, 1)

    def land(w, ryl, relays):
        for part in (0, 1):
            arrived(relays[part])
            core(w, ryl, 2, part)

    for r in range(4):
        other[r] = pack(4 + r)
    x_2 = send(other, block(1, 0, 0, 0), Y2)
    for r in range(4):
        xbuf[r, pl.ds(0, SLOTS), :] = pack(r)
    x_z0 = spread(0, 0)
    x_y0 = send(block(0, 0, 0, 0), block(0, 0, 1, 0), YN)
    core(0, 0, 0)

    upper, lower = pl.ds(0, 384), pl.ds(384, 384)

    def relay_weight(h):
        copies = []
        for k in (0, 1):
            arrived(w_x[h, k][0])
            copies.append(send(wgu.at[h, 3, upper, half[k]], wgu.at[h, 2, upper, half[k]], XP))
            arrived(w_x[h, k][1])
            copies.append(send(wgu.at[h, 1, lower, half[k]], wgu.at[h, 2, lower, half[k]], XM))
        return copies

    def partial(w, rz, h, dst, rows, shards=(0, 1, 3, 2), more=False):
        arrived(*from_core[w, rz])
        if 2 in shards:
            arrived(*(w_r0, w_r1)[h])

        @pl.loop(0, 2)
        def _(n):
            columns = pl.ds(pl.multiple_of(n * 256, 256), 256)
            at = pl.ds(w * ROWS + rz * 256, 256)
            into = pl.ds(pl.multiple_of(h * 512 + n * 256, 256), 256)
            total = dst[rows, into] if more else None
            for r in shards:
                part = jnp.dot(xbuf[r, at, :], wgu[h, r, :, columns], preferred_element_type=F32)
                total = part if total is None else total + part
            dst[rows, into] = total.astype(dst.dtype)

    def partial_out(rz, h):
        partial(1, rz, h, ps.at[rz], pl.ds(0, 256))

    def partial_own(rz, **kind):
        for h in (0, 1):
            partial(0, rz, h, acc, pl.ds(rz * 256, 256), **kind)

    def partial_last(rz):
        partial_own(rz, shards=(2,), more=True)

    row = lax.broadcasted_iota(jnp.int32, (2 * SLOTS, RUN), 0)
    picked = jnp.where(row >= SLOTS, row - SLOTS, row) == slot_row(ids_ref, slots_ref)
    weight = jnp.where(ids_ref[0:1, :] == 0, probs_ref[0:1, :], 0.0)
    weight += jnp.where(ids_ref[1:2, :] == 0, probs_ref[1:2, :], 0.0)
    picker_ref[...] = jnp.where(picked, 1.0, 0.0).T.astype(BF16)
    weight = jnp.sum(jnp.where(picked, weight, 0.0).T[:, :SLOTS], axis=1, keepdims=True)
    weight_ref[...] = jnp.broadcast_to(weight, (RUN, 2 * SLOTS))

    arrived(x_2)
    x_z1 = spread(1, 0)
    x_y1 = send(block(1, 0, 0, 0), block(1, 0, 1, 0), YN)
    d_y = send(wd_hbm, wd.at[4], Y2)
    core(1, 0, 0)
    both_cores(0, 0, x_z0)
    arrived(x_y0)
    x_yz0 = spread(0, 1)
    core(0, 1, 0)
    x_r1 = relay(1, 0, x_z1)
    both_cores(1, 0, x_z1)
    w_r0 = relay_weight(0)
    arrived(x_y1)
    x_yz1 = spread(1, 1)
    core(1, 1, 0)
    both_cores(0, 1, x_yz0)
    land(1, 0, x_r1)
    w_r1 = relay_weight(1)
    d_x = (send(wd_hbm, wd.at[3], XP), send(wd_hbm, wd.at[1], XM))
    for load in own_loads:
        load.wait()
    partial_own(0, shards=(0, 1, 3))
    partial_own(1, shards=(0, 1, 3))
    partial_own(3, shards=(0, 1, 3))
    x_yr1 = relay(1, 1, x_yz1)
    x_r0 = relay(0, 0, x_z0)
    x_yr0 = relay(0, 1, x_yz0)
    both_cores(1, 1, x_yz1)
    arrived(d_y)
    d_p = (send(wd.at[4], wd.at[7], XP), send(wd.at[4], wd.at[5], XM))
    partial_out(0, 0)
    land(1, 1, x_yr1)
    partial_out(1, 0)

    p = {(rz, ryl): [] for rz in range(4) for ryl in (0, 1)}

    def exchange(rz, ryl):
        at = pl.ds(ryl * 128, 128)
        p[rz, ryl].append(send(ps.at[rz, at], pr.at[rz, at], Y2))

    def hidden(rz, ryl):
        arrived(*p[rz, ryl])
        rows, at = pl.ds(rz * 256 + ryl * 128, 128), pl.ds(ryl * 128, 128)
        for h in (0, 1):
            g, u = pl.ds(h * 512, 256), pl.ds(h * 512 + 256, 256)
            gate = acc[rows, g] + pr[rz, at, g].astype(F32)
            up = acc[rows, u] + pr[rz, at, u].astype(F32)
            hid[rows, half[h]] = (gate / (1.0 + jnp.exp(-gate)) * up).astype(BF16)

    c1, z2, z1, y1, outs = {}, {}, {}, {}, {}
    slots, busy = [], set()

    def down(rz, ryl, first, count):
        if len(slots) % KEPT + count > KEPT:
            slots.extend([None] * (KEPT - len(slots) % KEPT))
        start = len(slots) % KEPT
        for j in range(count):
            if len(slots) + j >= KEPT and slots[len(slots) + j - KEPT] is not None:
                sent(slots[len(slots) + j - KEPT])
        assert busy.isdisjoint(range(start, start + count))
        busy.update(range(start, start + count))
        rows = pl.ds(rz * 256 + ryl * 128, 128)
        for j in range(count):
            part = jnp.dot(hid[rows, :], wd[ORDER[first + j]], preferred_element_type=F32)
            keep[start + j] = part[0:64]
            c1s[pl.ds((start + j) * 64, 64), :] = part[64:128].astype(BF16)
        copy = send(
            c1s.at[pl.ds(start * 64, count * 64)], c1r.at[rz * 2 + ryl, pl.ds(first * 64, count * 64)], CORE
        )
        slots.extend([copy] * count)
        c1[rz, ryl, first] = (copy, start, count)

    def sums(rz, ryl, first):
        copy, start, count = c1[rz, ryl, first]
        arrived(copy)
        for j in range(count):
            t = first + j
            total = keep[start + j] + c1r[rz * 2 + ryl, pl.ds(t * 64, 64), :].astype(F32)
            if t >= Y_FIRST:
                spot = Y_FIRST + (t - Y_FIRST) * 4 + rz
                if ryl == 1:
                    ys[spot] = total.astype(BF16)
                    y1[t, rz] = send(ys.at[spot], yr.at[spot], YN)
                    continue
                arrived(y1[t, rz])
                total += yr[spot].astype(F32)
            if rz == 0:
                q0[ryl, t] = total
            elif rz == 2:
                z2s[ryl, 0, t] = total[:, 0:384].astype(BF16)
                z2s[ryl, 1, t] = total[:, 384:768].astype(BF16)
            elif rz == 1:
                arrived(z2[ryl, 0, t])
                z1s[ryl, 0, t, :, 0:384] = (total[:, 0:384] + z2r[ryl, 0, t].astype(F32)).astype(BF16)
                z1s[ryl, 0, t, :, 384:768] = total[:, 384:768].astype(BF16)
            else:
                arrived(z2[ryl, 1, t])
                z1s[ryl, 1, t, :, 0:384] = total[:, 0:384].astype(BF16)
                z1s[ryl, 1, t, :, 384:768] = (total[:, 384:768] + z2r[ryl, 1, t].astype(F32)).astype(BF16)
        busy.difference_update(range(start, start + count))
        if first >= Y_FIRST and ryl == 1:
            return
        group = pl.ds(first, count)
        for way, to in ((0, ZP), (1, ZM)):
            if rz == 2:
                copy = send(z2s.at[ryl, way, group], z2r.at[ryl, way, group], to)
                for j in range(count):
                    z2[ryl, way, first + j] = copy
            elif rz == (1, 3)[way]:
                copy = send(z1s.at[ryl, way, group], z1r.at[ryl, way, group], to)
                for j in range(count):
                    z1[ryl, way, first + j] = copy

    def both(rz, ryl, first, count):
        down(rz, ryl, first, count)
        sums(rz, ryl, first)

    def over_z(ryl, t):
        arrived(z1[ryl, 0, t], z1[ryl, 1, t])
        return q0[ryl, t] + z1r[ryl, 0, t].astype(F32) + z1r[ryl, 1, t].astype(F32)

    def to_y(first, count):
        for t in range(first, first + count):
            ys[t] = over_z(1, t).astype(BF16)
        group = pl.ds(first, count)
        copy = send(ys.at[group], yr.at[group], YN)
        for t in range(first, first + count):
            y1[t] = copy

    def rows_out(first, count):
        for t in range(first, first + count):
            total = over_z(0, t)
            if t < Y_FIRST:
                arrived(y1[t])
                total += yr[t].astype(F32)
            head = total.astype(BF16)
            z1r[0, 0, t] = head
            z1r[0, 1, t] = (total - head.astype(F32)).astype(BF16)
            for part in (0, 1):
                outs[t, part] = pltpu.make_async_copy(
                    z1r.at[0, part, t],
                    out_hbm.at[pl.ds(part * SLOTS, SLOTS), shard_columns(ORDER[t])],
                    local_sem.at[13 + 2 * t + part],
                )
                outs[t, part].start()

    def relay_down(first, near, far, opposite):
        arrived(first[0])
        a = send(wd.at[near, half[0]], wd.at[far, half[0]], XP)
        arrived(first[1])
        return a, send(wd.at[opposite, half[1]], wd.at[far, half[1]], XM)

    partial_out(2, 0)
    early = send(ps.at[2, :, pl.ds(0, 512)], pr.at[2, :, pl.ds(0, 512)], Y2)
    land(0, 0, x_r0)
    land(0, 1, x_yr0)
    partial_out(3, 0)
    partial_out(2, 1)
    for ryl in (1, 0):
        at = pl.ds(ryl * 128, 128), pl.ds(512, 512)
        p[2, ryl] += [early, send(ps.at[2, at[0], at[1]], pr.at[2, at[0], at[1]], Y2)]
    partial_out(1, 1)
    exchange(1, 1)
    partial_out(3, 1)
    exchange(3, 1)
    exchange(1, 0)
    exchange(3, 0)
    partial_own(2)
    hidden(2, 1)
    down(2, 1, 0, 2)
    partial_last(1)
    sums(2, 1, 0)
    hidden(2, 0)
    down(2, 0, 0, 2)
    partial_out(0, 1)
    exchange(0, 1)
    exchange(0, 0)
    sums(2, 0, 0)
    hidden(1, 1)
    down(1, 1, 0, 2)
    d_r = relay_down(d_x, 3, 2, 1)
    down(2, 1, 2, 2)
    down(2, 0, 2, 2)
    sums(1, 1, 0)
    sums(2, 1, 2)
    sums(2, 0, 2)
    down(1, 1, 2, 2)
    partial_last(3)
    sums(1, 1, 2)
    hidden(3, 1)
    down(3, 1, 0, 4)
    partial_last(0)
    sums(3, 1, 0)
    hidden(1, 0)
    down(1, 0, 0, 4)
    sums(1, 0, 0)
    hidden(3, 0)
    down(3, 0, 0, 4)
    d_pr = relay_down(d_p, 7, 6, 5)
    down(2, 1, 4, 2)
    down(2, 0, 4, 2)
    sums(2, 1, 4)
    sums(2, 0, 4)
    sums(3, 0, 0)
    hidden(0, 1)
    down(0, 1, 0, 4)
    down(1, 1, 4, 2)
    down(3, 1, 4, 2)
    sums(0, 1, 0)
    sums(1, 1, 4)
    sums(3, 1, 4)
    down(1, 0, 4, 2)
    down(3, 0, 4, 2)
    to_y(0, 4)
    sums(1, 0, 4)
    sums(3, 0, 4)
    arrived(*d_r)
    down(2, 1, 6, 1)
    down(2, 0, 6, 1)
    hidden(0, 0)
    down(0, 0, 0, 4)
    sums(2, 1, 6)
    sums(2, 0, 6)
    down(0, 1, 4, 2)
    sums(0, 0, 0)
    for rz, ryl in ((1, 1), (3, 1), (1, 0), (3, 0)):
        down(rz, ryl, 6, 1)
    sums(0, 1, 4)
    arrived(*d_pr)
    for rz in (2, 3, 1, 0):
        down(rz, 1, 7, 1)
    for rz in (2, 3, 1, 0):
        sums(rz, 1, 7)
    for rz, ryl in ((1, 1), (3, 1), (1, 0), (3, 0)):
        sums(rz, ryl, 6)
    for rz in (2, 3, 1, 0):
        down(rz, 0, 7, 1)
    down(0, 0, 4, 2)
    down(0, 1, 6, 1)
    down(0, 0, 6, 1)
    sums(2, 0, 7)
    to_y(4, 2)
    sums(0, 0, 4)
    sums(0, 1, 6)
    sums(0, 0, 6)
    sums(3, 0, 7)
    sums(1, 0, 7)
    sums(0, 0, 7)
    to_y(6, 1)
    rows_out(0, 4)
    rows_out(4, 2)
    rows_out(7, 1)
    rows_out(6, 1)

    for copy in outs.values():
        copy.wait()
    for copy in left.values():
        copy.wait_send()
    assert len(started) <= COPIES


def body(tokens, expert_ids, slot_ids, gate_probs, gate_weight, up_weight, down_weight):
    hbm, vmem = pl.BlockSpec(memory_space=pl.ANY), pl.BlockSpec(memory_space=pltpu.VMEM)
    ids, slots, probs = expert_ids.T, slot_ids.T, gate_probs.T
    rows, picker, weight = pl.pallas_call(
        kernel,
        out_shape=(
            jax.ShapeDtypeStruct((2 * SLOTS, tokens.shape[1]), BF16),
            jax.ShapeDtypeStruct((RUN, 2 * SLOTS), BF16),
            jax.ShapeDtypeStruct((RUN, 2 * SLOTS), F32),
        ),
        in_specs=[hbm, vmem, vmem, vmem, hbm, hbm, hbm],
        out_specs=(hbm, vmem, vmem),
        scratch_shapes=[
            pltpu.VMEM((4, 2 * ROWS, DEPTH), BF16),
            pltpu.VMEM((4, SLOTS, DEPTH), BF16),
            pltpu.VMEM((2, 4, DEPTH, UNITS), BF16),
            pltpu.VMEM((SHARDS, UNITS, DEPTH), BF16),
            pltpu.VMEM((ROWS, 2 * UNITS), F32),
            pltpu.VMEM((4, 256, 2 * UNITS), BF16),
            pltpu.VMEM((4, 256, 2 * UNITS), BF16),
            pltpu.VMEM((ROWS, UNITS), BF16),
            pltpu.VMEM((KEPT * 64, DEPTH), BF16),
            pltpu.VMEM((KEPT, 64, DEPTH), F32),
            pltpu.VMEM((8, SHARDS * 64, DEPTH), BF16),
            pltpu.VMEM((2, 2, SHARDS, 64, 384), BF16),
            pltpu.VMEM((2, 2, SHARDS, 64, 384), BF16),
            pltpu.VMEM((2, 2, SHARDS, 64, DEPTH), BF16),
            pltpu.VMEM((2, 2, SHARDS, 64, DEPTH), BF16),
            pltpu.VMEM((2, SHARDS, 64, DEPTH), F32),
            pltpu.VMEM((Y_FIRST + (SHARDS - Y_FIRST) * 4, SLOTS, DEPTH), BF16),
            pltpu.VMEM((Y_FIRST + (SHARDS - Y_FIRST) * 4, SLOTS, DEPTH), BF16),
            pltpu.SemaphoreType.DMA((COPIES,)),
            pltpu.SemaphoreType.DMA((COPIES,)),
            pltpu.SemaphoreType.DMA((29,)),
        ],
        compiler_params=pltpu.CompilerParams(
            collective_id=0, has_side_effects=True, vmem_limit_bytes=62 << 20
        ),
        cost_estimate=pl.CostEstimate(flops=20_000_000_000, bytes_accessed=60_000_000, transcendentals=1_000_000),
    )(tokens, ids, slots, probs, gate_weight, up_weight, down_weight)
    small = pl.BlockSpec((RUN, 2 * SLOTS), lambda i: (0, 0))
    return pl.pallas_call(
        combine,
        grid=(2,),
        out_shape=jax.ShapeDtypeStruct(tokens.shape, BF16),
        in_specs=[small, small, pl.BlockSpec((2 * SLOTS, 4 * DEPTH), lambda i: (0, i))],
        out_specs=pl.BlockSpec((RUN, 4 * DEPTH), lambda i: (0, i)),
    )(picker, weight, rows)


def solution(mesh):
    return jax.shard_map(
        body,
        mesh=mesh,
        in_specs=(
            P(("dp", "tensor"), None),
            P(("dp", "tensor"), None),
            P(("dp", "tensor"), None),
            P(("dp", "tensor"), None),
            P("dp", "tensor"),
            P("dp", "tensor"),
            P("tensor", "dp"),
        ),
        out_specs=P(("dp", "tensor"), None),
        check_vma=False,
    )
```
